32 devices in a mesh: modes: 4 (over y, core), sites: 8 (over z, x).
Axes of the slice: x: 2, y: 2, z: 4, core: 2. Of those that a mesh axis runs over, the one named last changes fastest.
Arguments:
- wave_state: float32 [4, 32, 32768], P(None, 'modes', 'sites'), may hold values from -6 to 6
- potential: float32 [32768], P('sites'), may hold values from -0.5 to 0.5
- spin_angle: float32 [32768], P('sites'), may hold values from -3.140625 to 3.140625
- magnet: float32 [3, 32768], P(None, 'sites'), may hold values from -0.6 to 0.6
- magnetic_mask: int32 [32768], P('sites'), may hold values 0 or 1
- mode_weight: float32 [32], P('modes'), may hold values from 0.5 to 2
- source_amp: float32 [4, 32], P(None, 'modes'), may hold values from -6 to 6
- mode_group: int32 [32], P('modes'), may hold values from 0 to 7
- energies: float32 [8], replicated, may hold values from -2 to 2
- lead_site: int32 [32], P('modes'), may hold values from 0 to 32767
Outputs:
- next_state: float32 [4, 32, 32768], P(None, 'modes', 'sites')
- densities: float32 [5, 32768], P(None, 'sites')
- magnet_next: float32 [3, 32768], P(None, 'sites')
The draws below stay inside these ranges and needn't reach their ends.
All inputs are finite; a program needn't handle non-finite values. No bound on the sum of `magnetic_mask` on one device may be relied on, other than what follows from the above.
Results may differ from the reference program's by a relative error of at most 0.0001.
Values sent between devices are 32-bit elements; how exact they have to be, the bound alone decides.
No kernel may reach another device: no remote copies, remote signals or barrier semaphores. Data moves between devices by JAX's collectives and lax.ppermute only.
A program may use at most 64 MiB of HBM per device.

```python
import math
import jax
import jax.numpy as jnp
from jax import lax

MODE_DEV = 8
GROUPS = 8
MODES = 32
NSITES = 32768


def place_ends(entries, stream_key, smallest, top_value):
    longest = entries.shape.index(max(entries.shape))
    spots = []
    for shift in (0, 1):
        where = [jax.random.randint(jax.random.fold_in(stream_key, axis), (), 0, length) for axis, length in enumerate(entries.shape)]
        where[longest] = (where[longest] + shift) % entries.shape[longest]
        spots.append(tuple(where))
    return entries.at[spots[0]].set(smallest).at[spots[1]].set(top_value)


def block_scale(key, extent, pieces, least, largest):
    def one(position, blocks):
        steps = jax.random.uniform(jax.random.fold_in(jax.random.fold_in(key, 6), position), (blocks,), jnp.float32, least / len(pieces), largest / len(pieces))
        return jnp.repeat(jnp.exp(steps), extent[position] // blocks).reshape((-1,) + (1,) * (len(extent) - position - 1))

    loudness = one(*pieces[0])
    for cut in pieces[1:]:
        loudness = loudness * one(*cut)
    return loudness


def centred(stream_key, dims, scale, limit, shards=(), kind=jnp.bfloat16):
    entries = jax.random.normal(stream_key, dims, jnp.float32) * scale
    if len(shards) > 0:
        entries = block_scale(stream_key, dims, shards, -0.22, 0.18) * entries
    return jnp.clip(entries, min=-limit, max=limit).astype(kind)


def setup_inputs(seed: int = 0) -> dict:
    seeds = jax.random.split(jax.random.key(seed), 11)
    return {
        "wave_state": centred(seeds[0], (4, MODES, NSITES), 1.0, 6.0, ((1, 4), (2, 8)), jnp.float32),
        "potential": jnp.clip(jax.random.uniform(seeds[1], (NSITES,), jnp.float32, -0.5, 0.5) * block_scale(seeds[1], (NSITES,), ((0, 8),), -0.4, 0.0), -0.5, 0.5),
        "spin_angle": jnp.clip(jax.random.uniform(seeds[2], (NSITES,), jnp.float32, -3.140625, 3.140625), -3.140625, 3.140625),
        "magnet": jnp.clip(jax.random.uniform(seeds[3], (3, NSITES), jnp.float32, -0.6, 0.6) * block_scale(seeds[3], (3, NSITES), ((1, 8),), -0.4, 0.0), -0.6, 0.6),
        "magnetic_mask": place_ends((jax.random.randint(seeds[4], (NSITES,), 0, 2) < 1).astype(jnp.int32), jax.random.fold_in(seeds[4], 1), 0, 1),
        "mode_weight": jnp.clip(jnp.exp(math.log(2.0) - 1.3862944 * jax.random.uniform(seeds[5], (MODES,), jnp.float32) ** block_scale(seeds[5], (MODES,), ((0, 4),), -0.2, 0.2)), 0.5, 2.0),
        "source_amp": centred(seeds[6], (4, MODES), 1.0, 6.0, ((1, 4),), jnp.float32),
        "mode_group": place_ends(jax.random.randint(seeds[7], (MODES,), 0, GROUPS), jax.random.fold_in(seeds[7], 1), 0, GROUPS - 1).astype(jnp.int32),
        "energies": jnp.clip(jax.random.uniform(seeds[8], (GROUPS,), jnp.float32, -2.0, 2.0), -2.0, 2.0),
        "lead_site": place_ends(jax.random.randint(seeds[9], (MODES,), 0, NSITES), jax.random.fold_in(seeds[9], 1), 0, NSITES - 1).astype(jnp.int32),
    }


time_step = 0.6
start_time = 10.0
exchange_coupling = 0.5

def rotate_back(spinor, cosine, sine_term):
    shaped = spinor.reshape((2, 2) + spinor.shape[1:])
    spin_up = shaped[:, 0]
    spin_down = shaped[:, 1]
    turned = jnp.stack([cosine * spin_up + sine_term * spin_down, cosine * spin_down - sine_term * spin_up], axis=1)
    return turned.reshape(spinor.shape)

def rotate_fore(spinor, cosine, sine_term):
    shaped = spinor.reshape((2, 2) + spinor.shape[1:])
    spin_up = shaped[:, 0]
    spin_down = shaped[:, 1]
    turned = jnp.stack([cosine * spin_up - sine_term * spin_down, sine_term * spin_up + cosine * spin_down], axis=1)
    return turned.reshape(spinor.shape)

def exchange_term(spinor, sd_field):
    up_real, down_real, up_imag, down_imag = (spinor[0], spinor[1], spinor[2], spinor[3])
    field_x, field_y, field_z = (sd_field[0], sd_field[1], sd_field[2])
    out_up_real = field_z * up_real + field_x * down_real + field_y * down_imag
    out_down_real = field_x * up_real - field_y * up_imag - field_z * down_real
    out_up_imag = field_z * up_imag + field_x * down_imag - field_y * down_real
    out_down_imag = field_x * up_imag + field_y * up_real - field_z * down_imag
    return jnp.stack([out_up_real, out_down_real, out_up_imag, out_down_imag])

def source_field(offset, amplitude, energy, region):
    phase_angle = energy * (start_time + offset)
    cosine_phase = jnp.cos(phase_angle)
    sine_phase = jnp.sin(phase_angle)
    amp_real = amplitude[0:2]
    amp_imag = amplitude[2:4]
    real_part = amp_real * cosine_phase + amp_imag * sine_phase
    imag_part = amp_imag * cosine_phase - amp_real * sine_phase
    joined = jnp.concatenate([real_part, imag_part], axis=0)
    return joined[:, :, None] * region[None]

def rate(spinor, left_w, right_w, cosine, sine_term, potential, sd_field, source):
    hamil_term = potential * spinor + exchange_term(spinor, sd_field) - rotate_fore(left_w + right_w, cosine, sine_term) + source
    return jnp.concatenate([hamil_term[2:], -hamil_term[:2]], axis=0)

def densities_of(spinor, right_w, cosine, sine_term, weight_vec):
    up_real, down_real, up_imag, down_imag = (spinor[0], spinor[1], spinor[2], spinor[3])
    hopped = rotate_fore(right_w, cosine, sine_term)
    charge = up_real * up_real + down_real * down_real + up_imag * up_imag + down_imag * down_imag
    spin_x = 2.0 * (up_real * down_real + up_imag * down_imag)
    spin_y = 2.0 * (up_real * down_imag - up_imag * down_real)
    spin_z = up_real * up_real + up_imag * up_imag - down_real * down_real - down_imag * down_imag
    current = 2.0 * (up_real * hopped[2] + down_real * hopped[3] - up_imag * hopped[0] - down_imag * hopped[1])
    stacked = jnp.stack([charge, spin_x, spin_y, spin_z, current])
    return lax.optimization_barrier(jnp.sum(stacked * weight_vec[None, :, None], axis=1))

def advance(magnet, mask_float, totals):
    field_h = exchange_coupling * totals[1:4]
    torque = jnp.stack([magnet[1] * field_h[2] - magnet[2] * field_h[1], magnet[2] * field_h[0] - magnet[0] * field_h[2], magnet[0] * field_h[1] - magnet[1] * field_h[0]])
    return magnet - time_step * (mask_float * torque)

def reference(wave_state, potential, spin_angle, magnet, magnetic_mask, mode_weight, source_amp, mode_group, energies, lead_site):
    sites_all = wave_state.shape[2]
    modes_all = wave_state.shape[1]
    region_span = sites_all // 8
    cosine = jnp.cos(spin_angle)
    sine_term = jnp.sin(spin_angle)
    mask_float = magnetic_mask.astype(jnp.float32)
    sd_field = exchange_coupling * mask_float * magnet
    energy_all = lax.optimization_barrier(jnp.sum(jnp.where(mode_group[:, None] == jnp.arange(GROUPS, dtype=jnp.int32)[None, :], energies[None, :], jnp.zeros_like(energies)[None, :]), axis=1))
    positions = jnp.arange(sites_all, dtype=jnp.int32)
    block_size = MODE_DEV
    block_count = modes_all // block_size

    def one_block(block_index, state_pair):
        next_all, density_sum = state_pair
        offset_mode = (block_index * block_size).astype(jnp.int32)
        spinor = lax.dynamic_slice_in_dim(wave_state, offset_mode, block_size, 1)
        amplitude = lax.dynamic_slice_in_dim(source_amp, offset_mode, block_size, 1)
        energy = lax.dynamic_slice_in_dim(energy_all, offset_mode, block_size, 0)
        lead_block = lax.dynamic_slice_in_dim(lead_site, offset_mode, block_size, 0)
        weight_block = lax.dynamic_slice_in_dim(mode_weight, offset_mode, block_size, 0)
        region = ((positions[None, :] >= lead_block[:, None]) & (positions[None, :] < lead_block[:, None] + region_span)).astype(jnp.float32)

        def slope(spin_state, offset):
            weighted = rotate_back(spin_state, cosine, sine_term)
            padded = jnp.pad(weighted, ((0, 0), (0, 0), (1, 1)))
            source = source_field(offset, amplitude, energy, region)
            return (rate(spin_state, padded[..., :-2], padded[..., 2:], cosine, sine_term, potential, sd_field, source), padded)
        slope_one, padded_one = slope(spinor, 0.0)
        slope_two, ignored = slope(spinor + 0.5 * time_step * slope_one, 0.5 * time_step)
        slope_three, ignored = slope(spinor + 0.5 * time_step * slope_two, 0.5 * time_step)
        slope_four, ignored = slope(spinor + time_step * slope_three, time_step)
        advanced = spinor + time_step / 6.0 * (slope_one + 2.0 * slope_two + 2.0 * slope_three + slope_four)
        density_sum = density_sum + densities_of(spinor, padded_one[..., 2:], cosine, sine_term, weight_block)
        next_all = lax.dynamic_update_slice_in_dim(next_all, advanced, offset_mode, 1)
        return (next_all, density_sum)
    next_state, density_sum = lax.fori_loop(0, block_count, one_block, (jnp.zeros_like(wave_state), jnp.zeros((5, sites_all), jnp.float32)))
    root_scale = 1.0 / math.sqrt(modes_all)
    row_scale = jnp.array([1.0 / modes_all, root_scale, root_scale, root_scale, root_scale], jnp.float32)
    totals = density_sum * row_scale[:, None]
    magnet_next = advance(magnet, mask_float, totals)
    return (next_state, totals, magnet_next)
```

```python
import functools
import math

import jax
import jax.numpy as jnp
from jax import lax
from jax.experimental import pallas as pl
from jax.experimental.pallas import tpu as pltpu
from jax.sharding import PartitionSpec as P

time_step = 0.6
start_time = 10.0
exchange_coupling = 0.5
LANES = 128
SUBS = 8
STEP_COEF = (time_step / 4.0, time_step / 3.0, time_step / 2.0, time_step)
FIELD_ROWS = 8
PACK_ROWS = 4 * SUBS + FIELD_ROWS


def lane_iota():
    return lax.broadcasted_iota(jnp.int32, (SUBS, LANES), 1)


def sub_iota():
    return lax.broadcasted_iota(jnp.int32, (SUBS, LANES), 0)


def shift_from_left(tile):
    return pltpu.roll(tile, 1, 1)


def shift_from_right(tile):
    return pltpu.roll(tile, LANES - 1, 1)


def column(read):
    rows = sub_iota()
    out = jnp.full((SUBS, LANES), read(0))
    for mode in range(1, SUBS):
        out = jnp.where(rows == mode, read(mode), out)
    return out


def source_terms(parts, masked_cos, masked_sin):
    up_real, down_real, up_imag, down_imag = parts
    return (
        masked_cos * up_real + masked_sin * down_real,
        masked_cos * down_real - masked_sin * up_real,
        masked_cos * up_imag + masked_sin * down_imag,
        masked_cos * down_imag - masked_sin * up_imag,
    )


def horner(base, state, hops, fields, source, coef):
    up_real, down_real, up_imag, down_imag = state
    plus, minus, field_x, field_y = fields
    h_up_real = plus * up_real + field_x * down_real + field_y * down_imag - hops[0] + source[0]
    h_down_real = minus * down_real + field_x * up_real - field_y * up_imag - hops[1] + source[1]
    h_up_imag = plus * up_imag + field_x * down_imag - field_y * down_real - hops[2] + source[2]
    h_down_imag = minus * down_imag + field_x * up_imag + field_y * up_real - hops[3] + source[3]
    return (
        base[0] + coef * h_up_imag,
        base[1] + coef * h_down_imag,
        base[2] - coef * h_up_real,
        base[3] - coef * h_down_real,
    )


def prepare_kernel(
    all_modes,
    wave_ref,
    potential_ref,
    angle_ref,
    magnet_ref,
    mask_ref,
    weight_ref,
    amp_ref,
    group_ref,
    energies_ref,
    lead_ref,
    turned_ref,
    fields_ref,
    payload_ref,
    pack_a_ref,
    pack_b_ref,
    head_ref,
    tail_ref,
    source_ref,
):
    tiles = angle_ref.shape[0]
    lanes = lane_iota()
    site_index = lax.axis_index("sites")
    mode_index = lax.axis_index("modes")

    cosine = jnp.cos(angle_ref[...])
    sine = jnp.sin(angle_ref[...])
    fields_ref[4] = cosine
    fields_ref[5] = sine
    for part in range(3):
        for tile in range(tiles):
            fields_ref[part, tile : tile + 1, :] = magnet_ref[
                part : part + 1, tile * LANES : (tile + 1) * LANES
            ]
    strength = exchange_coupling * mask_ref[...].astype(jnp.float32)
    field_x = strength * fields_ref[0]
    field_y = strength * fields_ref[1]
    field_z = strength * fields_ref[2]
    cos_two = cosine * cosine - sine * sine
    sin_two = 2.0 * (cosine * sine)
    turned_z = field_z * cos_two + field_x * sin_two
    fields_ref[0] = potential_ref[...] + turned_z
    fields_ref[1] = potential_ref[...] - turned_z
    fields_ref[2] = field_x * cos_two - field_z * sin_two
    fields_ref[3] = field_y

    energy = column(lambda mode: energies_ref[group_ref[mode]])
    amps = [column(lambda mode, part=part: amp_ref[part, mode]) for part in range(4)]
    stages = []
    for offset in (0.0, 0.5 * time_step, time_step):
        phase = energy * (start_time + offset)
        cos_phase = jnp.cos(phase)
        sin_phase = jnp.sin(phase)
        stages.append(
            (
                amps[0] * cos_phase + amps[2] * sin_phase,
                amps[1] * cos_phase + amps[3] * sin_phase,
                amps[2] * cos_phase - amps[0] * sin_phase,
                amps[3] * cos_phase - amps[1] * sin_phase,
            )
        )
    first, middle, last = stages
    for part in range(4):
        combined = (
            first[part],
            0.5 * (first[part] + middle[part]),
            (first[part] + 2.0 * middle[part]) * (1.0 / 3.0),
            (first[part] + 4.0 * middle[part] + last[part]) * (1.0 / 6.0),
        )
        for step in range(4):
            source_ref[step * 4 + part] = combined[step]
    source_ref[16] = column(lambda mode: lead_ref[mode].astype(jnp.float32))

    weight = column(lambda mode: weight_ref[mode])
    charge_scale = 1.0 / all_modes
    spin_scale = 1.0 / math.sqrt(all_modes)

    def rotated(tile):
        at = pl.ds(pl.multiple_of(tile * LANES, LANES), LANES)
        cos_row = fields_ref[4, pl.ds(tile, 1), :]
        sin_row = fields_ref[5, pl.ds(tile, 1), :]
        up_real, down_real, up_imag, down_imag = (wave_ref[part, :, at] for part in range(4))
        out = (
            cos_row * up_real + sin_row * down_real,
            cos_row * down_real - sin_row * up_real,
            cos_row * up_imag + sin_row * down_imag,
            cos_row * down_imag - sin_row * up_imag,
        )
        for part in range(4):
            turned_ref[part, :, at] = out[part]
        return out

    def visit(tile, here, here_rolled, after_rolled, inside):
        at = pl.ds(pl.multiple_of(tile * LANES, LANES), LANES)
        up_real, down_real, up_imag, down_imag = (wave_ref[part, :, at] for part in range(4))
        follow = [jnp.where(lanes == LANES - 1, b, a) for a, b in zip(here_rolled, after_rolled)]
        up_square = up_real * up_real + up_imag * up_imag
        down_square = down_real * down_real + down_imag * down_imag
        current = (
            here[0] * follow[2] + here[1] * follow[3] - here[2] * follow[0] - here[3] * follow[1]
        )
        rows = (
            (up_square + down_square, charge_scale),
            (up_real * down_real + up_imag * down_imag, 2.0 * spin_scale),
            (up_real * down_imag - up_imag * down_real, 2.0 * spin_scale),
            (up_square - down_square, spin_scale),
            (current, 2.0 * spin_scale),
        )
        for place, (value, scale) in enumerate(rows):
            payload_ref[pl.ds(place * tiles + tile, 1), :] = scale * jnp.sum(
                value * weight, axis=0, keepdims=True
            )

    def body(tile, carry):
        here, here_rolled = carry
        after = rotated(tile + 1)
        after_rolled = tuple(shift_from_right(x) for x in after)
        visit(tile, here, here_rolled, after_rolled, True)
        return after, after_rolled

    begin = rotated(0)
    here, here_rolled = lax.fori_loop(
        0, tiles - 1, body, (begin, tuple(shift_from_right(x) for x in begin)), unroll=4
    )
    nothing = (jnp.zeros((SUBS, LANES), jnp.float32),) * 4
    visit(tiles - 1, here, here_rolled, nothing, False)

    slot = mode_index * 4
    scaled = (2.0 * spin_scale) * weight
    tails = jnp.zeros((SUBS, LANES), jnp.float32)
    heads = jnp.zeros((SUBS, LANES), jnp.float32)
    final = (tiles - 1) * LANES
    for part in range(4):
        tail_column = turned_ref[part, :, final + LANES - 1 : final + LANES]
        tails = jnp.where(lanes == slot + part, scaled * tail_column, tails)
        head_column = turned_ref[(part + 2) % 4, :, 0:1]
        head_column = head_column if part < 2 else -head_column
        heads = jnp.where(lanes == slot + part, head_column, heads)
    payload_ref[5 * tiles : 5 * tiles + SUBS, :] = tails
    payload_ref[5 * tiles + SUBS : 5 * tiles + 2 * SUBS, :] = heads

    for part in range(4):
        head_ref[part * SUBS : (part + 1) * SUBS, :] = turned_ref[part, :, 0:LANES]
        tail_ref[part * SUBS : (part + 1) * SUBS, :] = turned_ref[part, :, final : final + LANES]
    for part in range(6):
        head_ref[32 + part : 33 + part, :] = fields_ref[part, 0:1, :]
        tail_ref[32 + part : 33 + part, :] = fields_ref[part, tiles - 1 : tiles, :]
    ends = jnp.where(lax.broadcasted_iota(jnp.int32, (2, LANES), 0) == 0, 1.0, 0.0)
    head_ref[38:40, :] = ends
    tail_ref[38:40, :] = ends
    even = lax.rem(site_index, 2) == 0
    pack_a_ref[...] = jnp.where(even, tail_ref[...], head_ref[...])
    pack_b_ref[...] = jnp.where(even, head_ref[...], tail_ref[...])


def region_masks(positions, lead, span, cos_row, sin_row):
    offset = positions - lead
    inside = (offset >= 0.0) & (offset < span)
    zero = jnp.zeros((SUBS, LANES), jnp.float32)
    return jnp.where(inside, cos_row, zero), jnp.where(inside, sin_row, zero)


def interior_kernel(span, turned_ref, fields_ref, source_ref, next_ref, edge_ref, work_ref):
    tiles = fields_ref.shape[1]
    lanes = lane_iota()
    first_site = lax.axis_index("sites") * (tiles * LANES)
    lane_position = (lanes + first_site).astype(jnp.float32)
    lead = source_ref[16]
    zero = (jnp.zeros((SUBS, LANES), jnp.float32),) * 4

    for step in range(4):
        origin_ref = turned_ref if step == 0 else work_ref
        parts = [source_ref[step * 4 + part] for part in range(4)]

        def load(tile, origin_ref=origin_ref):
            at = pl.ds(pl.multiple_of(tile * LANES, LANES), LANES)
            return tuple(origin_ref[part, :, at] for part in range(4))

        def visit(tile, before_up, here, here_up, here_down, after_down, step=step, parts=parts):
            at = pl.ds(pl.multiple_of(tile * LANES, LANES), LANES)
            base = tuple(turned_ref[part, :, at] for part in range(4))
            rows = [fields_ref[place, pl.ds(tile, 1), :] for place in range(6)]
            hops = [
                jnp.where(lanes == 0, b, a) + jnp.where(lanes == LANES - 1, d, c)
                for a, b, c, d in zip(here_up, before_up, here_down, after_down)
            ]
            tile_start = lax.convert_element_type(tile * LANES, jnp.float32)
            masked = region_masks(lane_position + tile_start, lead, span, rows[4], rows[5])
            out = horner(
                base, here, hops, rows[:4], source_terms(parts, *masked), STEP_COEF[step]
            )
            if step == 3:
                out = (
                    rows[4] * out[0] - rows[5] * out[1],
                    rows[5] * out[0] + rows[4] * out[1],
                    rows[4] * out[2] - rows[5] * out[3],
                    rows[5] * out[2] + rows[4] * out[3],
                )
                for part in range(4):
                    next_ref[part, :, at] = out[part]
            else:
                for part in range(4):
                    work_ref[part, :, at] = out[part]

        def body(tile, carry, load=load, visit=visit):
            before_up, here, here_up, here_down = carry
            after = load(tile + 1)
            after_up = tuple(shift_from_left(x) for x in after)
            after_down = tuple(shift_from_right(x) for x in after)
            visit(tile, before_up, here, here_up, here_down, after_down)
            return here_up, after, after_up, after_down

        begin = load(0)
        carry = (
            zero,
            begin,
            tuple(shift_from_left(x) for x in begin),
            tuple(shift_from_right(x) for x in begin),
        )
        carry = lax.fori_loop(0, tiles - 1, body, carry, unroll=2)
        visit(tiles - 1, *carry, zero)

    final = (tiles - 1) * LANES
    for part in range(4):
        edge_ref[part] = next_ref[part, :, 0:LANES]
        edge_ref[4 + part] = next_ref[part, :, final : final + LANES]


def finish_kernel(
    span,
    mode_bits,
    *refs,
):
    (
        interior_ref,
        edge_ref,
        head_ref,
        tail_ref,
        recv_a_ref,
        recv_b_ref,
        source_ref,
        own_ref,
        other_ref,
        beyond_ref,
        beyond_other_ref,
        magnet_ref,
        mask_ref,
        next_ref,
        densities_ref,
        magnet_next_ref,
        patch_ref,
        sems,
    ) = refs
    tiles = mask_ref.shape[0]
    lanes = lane_iota()
    first_site = lax.axis_index("sites") * (tiles * LANES)
    even = lax.rem(lax.axis_index("sites"), 2) == 0
    lead = source_ref[16]
    final = (tiles - 1) * LANES
    half = LANES // 2

    left = jnp.where(even, recv_b_ref[...], recv_a_ref[...])
    right = jnp.where(even, recv_a_ref[...], recv_b_ref[...])
    upper = lax.broadcasted_iota(jnp.int32, (PACK_ROWS, LANES), 1) >= half
    patches = []
    for side, block in enumerate(
        (jnp.where(upper, left, head_ref[...]), jnp.where(upper, tail_ref[...], right))
    ):
        base = tuple(block[part * SUBS : (part + 1) * SUBS, :] for part in range(4))
        rows = [block[32 + place : 33 + place, :] for place in range(7)]
        if side == 0:
            position = first_site + jnp.where(lanes >= half, lanes - LANES, lanes)
        else:
            position = first_site + final + jnp.where(lanes >= half, lanes, lanes + LANES)
        masked = region_masks(position.astype(jnp.float32), lead, span, rows[4], rows[5])
        state = base
        for step in range(4):
            parts = [source_ref[step * 4 + part] for part in range(4)]
            hops = [shift_from_left(x) + shift_from_right(x) for x in state]
            state = horner(base, state, hops, rows[:4], source_terms(parts, *masked), STEP_COEF[step])
            state = tuple(rows[6] * x for x in state)
        out = (
            rows[4] * state[0] - rows[5] * state[1],
            rows[5] * state[0] + rows[4] * state[1],
            rows[4] * state[2] - rows[5] * state[3],
            rows[5] * state[2] + rows[4] * state[3],
        )
        fresh = lanes < 4 if side == 0 else lanes >= LANES - 4
        for part in range(4):
            patch_ref[side, part] = jnp.where(fresh, out[part], edge_ref[side * 4 + part])
    copies = [
        pltpu.make_async_copy(
            patch_ref.at[side],
            next_ref.at[:, :, pl.ds(side * final, LANES)],
            sems.at[side],
        )
        for side in range(2)
    ]
    for copy in copies:
        copy.start()

    for place in range(5):
        rows = pl.ds(place * tiles, tiles)
        total = own_ref[rows, :] + other_ref[rows, :]
        if place == 4:
            ends = pl.ds(5 * tiles, SUBS)
            tails = own_ref[ends, :] + other_ref[ends, :]
            heads = beyond_ref[...] + beyond_other_ref[...]
            corner = jnp.sum(jnp.sum(tails * heads, axis=1, keepdims=True), axis=0, keepdims=True)
            row_at = lax.broadcasted_iota(jnp.int32, (tiles, LANES), 0)
            lane_at = lax.broadcasted_iota(jnp.int32, (tiles, LANES), 1)
            total = jnp.where((row_at == tiles - 1) & (lane_at == LANES - 1), corner, total)
        for tile in range(tiles):
            densities_ref[place : place + 1, tile * LANES : (tile + 1) * LANES] = total[
                tile : tile + 1, :
            ]
    for tile in range(tiles):
        at = slice(tile * LANES, (tile + 1) * LANES)
        mask_row = mask_ref[tile : tile + 1, :].astype(jnp.float32)
        field_x, field_y, field_z = (
            exchange_coupling * densities_ref[1 + part : 2 + part, at] for part in range(3)
        )
        magnet_x, magnet_y, magnet_z = (magnet_ref[part : part + 1, at] for part in range(3))
        torque = (
            magnet_y * field_z - magnet_z * field_y,
            magnet_z * field_x - magnet_x * field_z,
            magnet_x * field_y - magnet_y * field_x,
        )
        for part, magnet in enumerate((magnet_x, magnet_y, magnet_z)):
            magnet_next_ref[part : part + 1, at] = magnet - time_step * (mask_row * torque[part])

    for copy in copies:
        copy.wait()


def local(
    wave_state,
    potential,
    spin_angle,
    magnet,
    magnetic_mask,
    mode_weight,
    source_amp,
    mode_group,
    energies,
    lead_site,
):
    local_modes, local_sites = wave_state.shape[1:]
    site_count = lax.axis_size("sites")
    mode_count = lax.axis_size("modes")
    assert local_modes == SUBS and local_sites % LANES == 0
    tiles = local_sites // LANES
    span = float(local_sites * site_count // 8)
    f32 = jnp.float32
    vmem = pl.BlockSpec(memory_space=pltpu.VMEM)
    smem = pl.BlockSpec(memory_space=pltpu.SMEM)
    anywhere = pl.BlockSpec(memory_space=pl.ANY)
    dense = (tiles, LANES)
    payload_rows = 5 * tiles + 2 * SUBS

    turned, fields, payload, pack_a, pack_b, head, tail, source = pl.pallas_call(
        functools.partial(prepare_kernel, local_modes * mode_count),
        out_shape=(
            jax.ShapeDtypeStruct(wave_state.shape, f32),
            jax.ShapeDtypeStruct((6,) + dense, f32),
            jax.ShapeDtypeStruct((payload_rows, LANES), f32),
            jax.ShapeDtypeStruct((PACK_ROWS, LANES), f32),
            jax.ShapeDtypeStruct((PACK_ROWS, LANES), f32),
            jax.ShapeDtypeStruct((PACK_ROWS, LANES), f32),
            jax.ShapeDtypeStruct((PACK_ROWS, LANES), f32),
            jax.ShapeDtypeStruct((17, SUBS, LANES), f32),
        ),
        in_specs=[vmem] * 5 + [smem] * 5,
        out_specs=[vmem] * 8,
        name="prepare",
        cost_estimate=pl.CostEstimate(flops=10_000_000, bytes_accessed=1_500_000, transcendentals=0),
    )(
        wave_state,
        potential.reshape(dense),
        spin_angle.reshape(dense),
        magnet,
        magnetic_mask.reshape(dense),
        mode_weight,
        source_amp,
        mode_group,
        energies,
        lead_site,
    )

    pairs_a = [(i, i + 1) for i in range(0, site_count - 1, 2)]
    pairs_b = [(i, i + 1) for i in range(1, site_count - 1, 2)]
    both = lambda pairs: pairs + [(j, i) for i, j in pairs]
    recv_b = lax.ppermute(pack_b, "sites", both(pairs_b))
    recv_a = lax.ppermute(pack_a, "sites", both(pairs_a))

    own = payload
    distance = 1
    while 2 * distance < mode_count:
        own = own + lax.ppermute(own, "modes", [(i, i ^ distance) for i in range(mode_count)])
        distance *= 2
    other = lax.ppermute(own, "modes", [(i, i ^ distance) for i in range(mode_count)])

    heads = slice(5 * tiles + SUBS, payload_rows)
    to_left = [(i + 1, i) for i in range(site_count - 1)]
    beyond = lax.ppermute(own[heads] + other[heads], "sites", to_left)
    beyond_other = jnp.zeros_like(beyond)

    interior, edge = pl.pallas_call(
        functools.partial(interior_kernel, span),
        out_shape=(
            jax.ShapeDtypeStruct(wave_state.shape, f32),
            jax.ShapeDtypeStruct((8, SUBS, LANES), f32),
        ),
        in_specs=[vmem] * 3,
        out_specs=[vmem] * 2,
        scratch_shapes=[pltpu.VMEM(wave_state.shape, f32)],
        name="interior",
        cost_estimate=pl.CostEstimate(flops=20_000_000, bytes_accessed=1_500_000, transcendentals=0),
    )(turned, fields, source)

    next_state, densities, magnet_next = pl.pallas_call(
        functools.partial(finish_kernel, span, mode_count),
        out_shape=(
            jax.ShapeDtypeStruct(wave_state.shape, f32),
            jax.ShapeDtypeStruct((5, local_sites), f32),
            jax.ShapeDtypeStruct((3, local_sites), f32),
        ),
        in_specs=[anywhere] + [vmem] * 12,
        out_specs=[anywhere, vmem, vmem],
        scratch_shapes=[
            pltpu.VMEM((2, 4, SUBS, LANES), f32),
            pltpu.SemaphoreType.DMA((2,)),
        ],
        input_output_aliases={0: 0},
        name="finish",
        cost_estimate=pl.CostEstimate(flops=1_000_000, bytes_accessed=400_000, transcendentals=0),
    )(
        interior,
        edge,
        head,
        tail,
        recv_a,
        recv_b,
        source,
        own,
        other,
        beyond,
        beyond_other,
        magnet,
        magnetic_mask.reshape(dense),
    )
    return (next_state, densities, magnet_next)


def solution(mesh):
    return jax.shard_map(
        local,
        mesh=mesh,
        in_specs=(
            P(None, "modes", "sites"),
            P("sites"),
            P("sites"),
            P(None, "sites"),
            P("sites"),
            P("modes"),
            P(None, "modes"),
            P("modes"),
            P(),
            P("modes"),
        ),
        out_specs=(P(None, "modes", "sites"), P(None, "sites"), P(None, "sites")),
        check_vma=False,
    )
```

```python
import functools
import math

import jax
import jax.numpy as jnp
from jax import lax
from jax.experimental import pallas as pl
from jax.experimental.pallas import tpu as pltpu
from jax.sharding import PartitionSpec as P

time_step = 0.6
start_time = 10.0
exchange_coupling = 0.5
LANES = 128
SUBS = 8
PIECES = 4
STEP_COEF = (time_step / 4.0, time_step / 3.0, time_step / 2.0, time_step)
FIELD_ROWS = 8
PACK_ROWS = 4 * SUBS + FIELD_ROWS


def lane_iota():
    return lax.broadcasted_iota(jnp.int32, (SUBS, LANES), 1)


def sub_iota():
    return lax.broadcasted_iota(jnp.int32, (SUBS, LANES), 0)


def shift_from_left(tile):
    return pltpu.roll(tile, 1, 1)


def shift_from_right(tile):
    return pltpu.roll(tile, LANES - 1, 1)


def column(read):
    rows = sub_iota()
    out = jnp.full((SUBS, LANES), read(0))
    for mode in range(1, SUBS):
        out = jnp.where(rows == mode, read(mode), out)
    return out


def source_terms(parts, masked_cos, masked_sin):
    up_real, down_real, up_imag, down_imag = parts
    return (
        masked_cos * up_real + masked_sin * down_real,
        masked_cos * down_real - masked_sin * up_real,
        masked_cos * up_imag + masked_sin * down_imag,
        masked_cos * down_imag - masked_sin * up_imag,
    )


def rotate_fore(state, cos_row, sin_row):
    return (
        cos_row * state[0] - sin_row * state[1],
        sin_row * state[0] + cos_row * state[1],
        cos_row * state[2] - sin_row * state[3],
        sin_row * state[2] + cos_row * state[3],
    )


def horner(base, state, hops, fields, source, coef):
    up_real, down_real, up_imag, down_imag = state
    plus, minus, field_x, field_y = fields
    h_up_real = plus * up_real + field_x * down_real + field_y * down_imag - hops[0] + source[0]
    h_down_real = minus * down_real + field_x * up_real - field_y * up_imag - hops[1] + source[1]
    h_up_imag = plus * up_imag + field_x * down_imag - field_y * down_real - hops[2] + source[2]
    h_down_imag = minus * down_imag + field_x * up_imag + field_y * up_real - hops[3] + source[3]
    return (
        base[0] + coef * h_up_imag,
        base[1] + coef * h_down_imag,
        base[2] - coef * h_up_real,
        base[3] - coef * h_down_real,
    )


def prepare_kernel(
    all_modes,
    wave_ref,
    potential_ref,
    angle_ref,
    magnet_ref,
    mask_ref,
    weight_ref,
    amp_ref,
    group_ref,
    energies_ref,
    lead_ref,
    turned_ref,
    fields_ref,
    payload_ref,
    pack_a_ref,
    pack_b_ref,
    source_ref,
    spin_ref,
    wave_in,
    sems,
):
    tiles = angle_ref.shape[0]
    piece = tiles * LANES // PIECES
    copies = [
        pltpu.make_async_copy(
            wave_ref.at[:, :, pl.ds(part * piece, piece)],
            wave_in.at[:, :, pl.ds(part * piece, piece)],
            sems.at[part],
        )
        for part in range(PIECES)
    ]
    for copy in copies:
        copy.start()

    lanes = lane_iota()
    site_index = lax.axis_index("sites")
    mode_index = lax.axis_index("modes")

    cosine = jnp.cos(angle_ref[...])
    sine = jnp.sin(angle_ref[...])
    fields_ref[4] = cosine
    fields_ref[5] = sine
    for part in range(3):
        for tile in range(tiles):
            spin_ref[part, tile : tile + 1, :] = magnet_ref[
                part : part + 1, tile * LANES : (tile + 1) * LANES
            ]
    mask = mask_ref[...].astype(jnp.float32)
    strength = exchange_coupling * mask
    field_x = strength * spin_ref[0]
    field_y = strength * spin_ref[1]
    field_z = strength * spin_ref[2]
    cos_two = cosine * cosine - sine * sine
    sin_two = 2.0 * (cosine * sine)
    turned_z = field_z * cos_two + field_x * sin_two
    fields_ref[0] = potential_ref[...] + turned_z
    fields_ref[1] = potential_ref[...] - turned_z
    fields_ref[2] = field_x * cos_two - field_z * sin_two
    fields_ref[3] = field_y
    spin_ref[3] = time_step * mask

    energy = column(lambda mode: energies_ref[group_ref[mode]])
    amps = [column(lambda mode, part=part: amp_ref[part, mode]) for part in range(4)]
    stages = []
    for offset in (0.0, 0.5 * time_step, time_step):
        phase = energy * (start_time + offset)
        cos_phase = jnp.cos(phase)
        sin_phase = jnp.sin(phase)
        stages.append(
            (
                amps[0] * cos_phase + amps[2] * sin_phase,
                amps[1] * cos_phase + amps[3] * sin_phase,
                amps[2] * cos_phase - amps[0] * sin_phase,
                amps[3] * cos_phase - amps[1] * sin_phase,
            )
        )
    first, middle, last = stages
    for part in range(4):
        combined = (
            first[part],
            0.5 * (first[part] + middle[part]),
            (first[part] + 2.0 * middle[part]) * (1.0 / 3.0),
            (first[part] + 4.0 * middle[part] + last[part]) * (1.0 / 6.0),
        )
        for step in range(4):
            source_ref[step * 4 + part] = combined[step]
    source_ref[16] = column(lambda mode: lead_ref[mode].astype(jnp.float32))

    weight = column(lambda mode: weight_ref[mode])
    charge_scale = 1.0 / all_modes
    spin_scale = 1.0 / math.sqrt(all_modes)
    nothing = (jnp.zeros((SUBS, LANES), jnp.float32),) * 4

    def rotated(tile):
        if tile == tiles:
            return nothing
        at = slice(tile * LANES, (tile + 1) * LANES)
        if tile * LANES % piece == 0:
            copies[tile * LANES // piece].wait()
        cos_row = fields_ref[4, tile : tile + 1, :]
        sin_row = fields_ref[5, tile : tile + 1, :]
        up_real, down_real, up_imag, down_imag = (wave_in[part, :, at] for part in range(4))
        out = (
            cos_row * up_real + sin_row * down_real,
            cos_row * down_real - sin_row * up_real,
            cos_row * up_imag + sin_row * down_imag,
            cos_row * down_imag - sin_row * up_imag,
        )
        for part in range(4):
            turned_ref[part, :, at] = out[part]
        return out

    here = rotated(0)
    here_rolled = [shift_from_right(x) for x in here]
    for tile in range(tiles):
        at = slice(tile * LANES, (tile + 1) * LANES)
        after = rotated(tile + 1)
        after_rolled = [shift_from_right(x) for x in after]
        up_real, down_real, up_imag, down_imag = (wave_in[part, :, at] for part in range(4))
        follow = [jnp.where(lanes == LANES - 1, b, a) for a, b in zip(here_rolled, after_rolled)]
        up_square = up_real * up_real + up_imag * up_imag
        down_square = down_real * down_real + down_imag * down_imag
        current = (
            here[0] * follow[2] + here[1] * follow[3] - here[2] * follow[0] - here[3] * follow[1]
        )
        rows = (
            (up_square + down_square, charge_scale),
            (up_real * down_real + up_imag * down_imag, 2.0 * spin_scale),
            (up_real * down_imag - up_imag * down_real, 2.0 * spin_scale),
            (up_square - down_square, spin_scale),
            (current, 2.0 * spin_scale),
        )
        for place, (value, scale) in enumerate(rows):
            payload_ref[place * tiles + tile : place * tiles + tile + 1, :] = scale * jnp.sum(
                value * weight, axis=0, keepdims=True
            )
        here, here_rolled = after, after_rolled

    slot = mode_index * 4
    scaled = (2.0 * spin_scale) * weight
    tails = jnp.zeros((SUBS, LANES), jnp.float32)
    heads = jnp.zeros((SUBS, LANES), jnp.float32)
    final = (tiles - 1) * LANES
    for part in range(4):
        tail_column = turned_ref[part, :, final + LANES - 1 : final + LANES]
        tails = jnp.where(lanes == slot + part, scaled * tail_column, tails)
        head_column = turned_ref[(part + 2) % 4, :, 0:1]
        head_column = head_column if part < 2 else -head_column
        heads = jnp.where(lanes == slot + part, head_column, heads)
    payload_ref[5 * tiles : 5 * tiles + SUBS, :] = tails
    payload_ref[5 * tiles + SUBS : 5 * tiles + 2 * SUBS, :] = heads

    even = lax.rem(site_index, 2) == 0
    for part in range(4):
        at = slice(part * SUBS, (part + 1) * SUBS)
        head = turned_ref[part, :, 0:LANES]
        tail = turned_ref[part, :, final : final + LANES]
        pack_a_ref[at, :] = jnp.where(even, tail, head)
        pack_b_ref[at, :] = jnp.where(even, head, tail)
    for place in range(6):
        at = slice(32 + place, 33 + place)
        head = fields_ref[place, 0:1, :]
        tail = fields_ref[place, tiles - 1 : tiles, :]
        pack_a_ref[at, :] = jnp.where(even, tail, head)
        pack_b_ref[at, :] = jnp.where(even, head, tail)
    ends = jnp.where(lax.broadcasted_iota(jnp.int32, (2, LANES), 0) == 0, 1.0, 0.0)
    pack_a_ref[38:40, :] = ends
    pack_b_ref[38:40, :] = ends


def region_masks(positions, lead, span, cos_row, sin_row):
    offset = positions - lead
    inside = (offset >= 0.0) & (offset < span)
    zero = jnp.zeros((SUBS, LANES), jnp.float32)
    return jnp.where(inside, cos_row, zero), jnp.where(inside, sin_row, zero)


def interior_kernel(span, turned_ref, fields_ref, source_ref, next_ref, edge_ref, *scratch):
    (work_a, work_b, out_ref, sems) = scratch
    tiles = fields_ref.shape[1]
    piece = tiles * LANES // PIECES
    lanes = lane_iota()
    first_site = lax.axis_index("sites") * (tiles * LANES)
    lane_position = (lanes + first_site).astype(jnp.float32)
    lead = source_ref[16]
    zero = (jnp.zeros((SUBS, LANES), jnp.float32),) * 4
    targets = (work_a, work_b, work_a, out_ref)
    copies = [
        pltpu.make_async_copy(
            out_ref.at[:, :, pl.ds(part * piece, piece)],
            next_ref.at[:, :, pl.ds(part * piece, piece)],
            sems.at[part],
        )
        for part in range(PIECES)
    ]

    for step in range(4):
        origin_ref = turned_ref if step == 0 else targets[step - 1]
        target_ref = targets[step]
        parts = [source_ref[step * 4 + part] for part in range(4)]

        def load(tile):
            if tile == tiles:
                return zero
            return tuple(
                origin_ref[part, :, tile * LANES : (tile + 1) * LANES] for part in range(4)
            )

        before_up = zero
        here = load(0)
        here_up = [shift_from_left(x) for x in here]
        here_down = [shift_from_right(x) for x in here]
        for tile in range(tiles):
            at = slice(tile * LANES, (tile + 1) * LANES)
            after = load(tile + 1)
            after_up = [shift_from_left(x) for x in after]
            after_down = [shift_from_right(x) for x in after]
            base = tuple(turned_ref[part, :, at] for part in range(4))
            rows = [fields_ref[place, tile : tile + 1, :] for place in range(6)]
            hops = [
                jnp.where(lanes == 0, b, a) + jnp.where(lanes == LANES - 1, d, c)
                for a, b, c, d in zip(here_up, before_up, here_down, after_down)
            ]
            masked = region_masks(
                lane_position + float(tile * LANES), lead, span, rows[4], rows[5]
            )
            out = horner(
                base, here, hops, rows[:4], source_terms(parts, *masked), STEP_COEF[step]
            )
            if step == 3:
                out = rotate_fore(out, rows[4], rows[5])
            for part in range(4):
                target_ref[part, :, at] = out[part]
            if step == 3 and (tile + 1) * LANES % piece == 0:
                copies[tile * LANES // piece].start()
            before_up, here, here_up, here_down = here_up, after, after_up, after_down

    final = (tiles - 1) * LANES
    for part in range(4):
        edge_ref[part] = out_ref[part, :, 0:LANES]
        edge_ref[4 + part] = out_ref[part, :, final : final + LANES]
    for copy in copies:
        copy.wait()


def finish_kernel(span, *refs):
    (
        interior_ref,
        edge_ref,
        turned_ref,
        fields_ref,
        recv_a_ref,
        recv_b_ref,
        source_ref,
        own_ref,
        other_ref,
        beyond_ref,
        beyond_other_ref,
        spin_ref,
        next_ref,
        densities_ref,
        magnet_next_ref,
        patch_ref,
        sems,
    ) = refs
    tiles = fields_ref.shape[1]
    lanes = lane_iota()
    first_site = lax.axis_index("sites") * (tiles * LANES)
    even = lax.rem(lax.axis_index("sites"), 2) == 0
    lead = source_ref[16]
    final = (tiles - 1) * LANES
    half = LANES // 2
    upper = lanes >= half
    upper_row = upper[0:1, :]

    for side in range(2):
        near, far = (recv_b_ref, recv_a_ref) if side == 0 else (recv_a_ref, recv_b_ref)

        def joined(pack_at, own, upper_half):
            fetched = jnp.where(even, near[pack_at, :], far[pack_at, :])
            if side == 0:
                return jnp.where(upper_half, fetched, own)
            return jnp.where(upper_half, own, fetched)

        edge_tile = 0 if side == 0 else tiles - 1
        at = slice(edge_tile * LANES, (edge_tile + 1) * LANES)
        base = tuple(
            joined(slice(part * SUBS, (part + 1) * SUBS), turned_ref[part, :, at], upper)
            for part in range(4)
        )
        rows = [
            joined(
                slice(32 + place, 33 + place),
                fields_ref[place, edge_tile : edge_tile + 1, :],
                upper_row,
            )
            for place in range(6)
        ]
        inside = joined(slice(38, 39), jnp.ones((1, LANES), jnp.float32), upper_row)
        if side == 0:
            position = first_site + jnp.where(upper, lanes - LANES, lanes)
        else:
            position = first_site + final + jnp.where(upper, lanes, lanes + LANES)
        masked = region_masks(position.astype(jnp.float32), lead, span, rows[4], rows[5])
        state = base
        for step in range(4):
            parts = [source_ref[step * 4 + part] for part in range(4)]
            hops = [shift_from_left(x) + shift_from_right(x) for x in state]
            state = horner(base, state, hops, rows[:4], source_terms(parts, *masked), STEP_COEF[step])
            if step < 3:
                state = tuple(inside * x for x in state)
        out = rotate_fore(state, rows[4], rows[5])
        fresh = lanes < 4 if side == 0 else lanes >= LANES - 4
        for part in range(4):
            patch_ref[side, part] = jnp.where(fresh, out[part], edge_ref[side * 4 + part])
    copies = [
        pltpu.make_async_copy(
            patch_ref.at[side],
            next_ref.at[:, :, pl.ds(side * final, LANES)],
            sems.at[side],
        )
        for side in range(2)
    ]
    for copy in copies:
        copy.start()

    totals = []
    for place in range(5):
        rows = slice(place * tiles, (place + 1) * tiles)
        totals.append(own_ref[rows, :] + other_ref[rows, :])
    ends = slice(5 * tiles, 5 * tiles + SUBS)
    tails = own_ref[ends, :] + other_ref[ends, :]
    heads = beyond_ref[...] + beyond_other_ref[...]
    corner = jnp.sum(jnp.sum(tails * heads, axis=1, keepdims=True), axis=0, keepdims=True)
    row_at = lax.broadcasted_iota(jnp.int32, (tiles, LANES), 0)
    lane_at = lax.broadcasted_iota(jnp.int32, (tiles, LANES), 1)
    totals[4] = jnp.where((row_at == tiles - 1) & (lane_at == LANES - 1), corner, totals[4])
    for place in range(5):
        for tile in range(tiles):
            densities_ref[place : place + 1, tile * LANES : (tile + 1) * LANES] = totals[place][
                tile : tile + 1, :
            ]
    field_x, field_y, field_z = (exchange_coupling * totals[1 + part] for part in range(3))
    magnet_x, magnet_y, magnet_z = (spin_ref[part] for part in range(3))
    torque = (
        magnet_y * field_z - magnet_z * field_y,
        magnet_z * field_x - magnet_x * field_z,
        magnet_x * field_y - magnet_y * field_x,
    )
    for part, magnet in enumerate((magnet_x, magnet_y, magnet_z)):
        advanced = magnet - spin_ref[3] * torque[part]
        for tile in range(tiles):
            magnet_next_ref[part : part + 1, tile * LANES : (tile + 1) * LANES] = advanced[
                tile : tile + 1, :
            ]

    for copy in copies:
        copy.wait()


def local(
    wave_state,
    potential,
    spin_angle,
    magnet,
    magnetic_mask,
    mode_weight,
    source_amp,
    mode_group,
    energies,
    lead_site,
):
    local_modes, local_sites = wave_state.shape[1:]
    site_count = lax.axis_size("sites")
    mode_count = lax.axis_size("modes")
    assert local_modes == SUBS and local_sites % (LANES * PIECES) == 0
    tiles = local_sites // LANES
    span = float(local_sites * site_count // 8)
    f32 = jnp.float32
    vmem = pl.BlockSpec(memory_space=pltpu.VMEM)
    smem = pl.BlockSpec(memory_space=pltpu.SMEM)
    anywhere = pl.BlockSpec(memory_space=pl.ANY)
    dense = (tiles, LANES)
    payload_rows = 5 * tiles + 2 * SUBS
    kept = lambda array: pltpu.with_memory_space_constraint(array, pltpu.VMEM)

    turned, fields, payload, pack_a, pack_b, source, spin = pl.pallas_call(
        functools.partial(prepare_kernel, local_modes * mode_count),
        out_shape=(
            pltpu.VMEM(wave_state.shape, f32),
            pltpu.VMEM((6,) + dense, f32),
            pltpu.VMEM((payload_rows, LANES), f32),
            pltpu.VMEM((PACK_ROWS, LANES), f32),
            pltpu.VMEM((PACK_ROWS, LANES), f32),
            pltpu.VMEM((17, SUBS, LANES), f32),
            pltpu.VMEM((4,) + dense, f32),
        ),
        in_specs=[anywhere] + [vmem] * 4 + [smem] * 5,
        out_specs=[vmem] * 7,
        scratch_shapes=[
            pltpu.VMEM(wave_state.shape, f32),
            pltpu.SemaphoreType.DMA((PIECES,)),
        ],
        name="prepare",
        cost_estimate=pl.CostEstimate(flops=10_000_000, bytes_accessed=1_500_000, transcendentals=0),
    )(
        wave_state,
        potential.reshape(dense),
        spin_angle.reshape(dense),
        magnet,
        magnetic_mask.reshape(dense),
        mode_weight,
        source_amp,
        mode_group,
        energies,
        lead_site,
    )

    own = payload
    distance = 1
    while 2 * distance < mode_count:
        own = own + lax.ppermute(own, "modes", [(i, i ^ distance) for i in range(mode_count)])
        distance *= 2

    pairs_a = [(i, i + 1) for i in range(0, site_count - 1, 2)]
    pairs_b = [(i, i + 1) for i in range(1, site_count - 1, 2)]
    both = lambda pairs: pairs + [(j, i) for i, j in pairs]
    recv_b = lax.ppermute(pack_b, "sites", both(pairs_b))
    recv_a = lax.ppermute(pack_a, "sites", both(pairs_a))

    other = lax.ppermute(own, "modes", [(i, i ^ distance) for i in range(mode_count)])
    first_sites = slice(5 * tiles + SUBS, payload_rows)
    if mode_count == 4:
        across = [
            (((m if m % 2 == 0 else m ^ 2) * site_count + s + 1), m * site_count + s)
            for m in range(mode_count)
            for s in range(site_count - 1)
        ]
        beyond = lax.ppermute(own[first_sites], ("modes", "sites"), across)
        beyond_other = lax.ppermute(beyond, "modes", [(i, i ^ 1) for i in range(mode_count)])
    else:
        to_left = [(i + 1, i) for i in range(site_count - 1)]
        beyond = lax.ppermute(own[first_sites] + other[first_sites], "sites", to_left)
        beyond_other = jnp.zeros_like(beyond)

    interior, edge = pl.pallas_call(
        functools.partial(interior_kernel, span),
        out_shape=(
            jax.ShapeDtypeStruct(wave_state.shape, f32),
            pltpu.VMEM((8, SUBS, LANES), f32),
        ),
        in_specs=[vmem] * 3,
        out_specs=[anywhere, vmem],
        scratch_shapes=[pltpu.VMEM(wave_state.shape, f32)] * 3
        + [pltpu.SemaphoreType.DMA((PIECES,))],
        name="interior",
        cost_estimate=pl.CostEstimate(flops=20_000_000, bytes_accessed=1_500_000, transcendentals=0),
    )(kept(turned), kept(fields), kept(source))

    next_state, densities, magnet_next = pl.pallas_call(
        functools.partial(finish_kernel, span),
        out_shape=(
            jax.ShapeDtypeStruct(wave_state.shape, f32),
            jax.ShapeDtypeStruct((5, local_sites), f32),
            jax.ShapeDtypeStruct((3, local_sites), f32),
        ),
        in_specs=[anywhere] + [vmem] * 11,
        out_specs=[anywhere, vmem, vmem],
        scratch_shapes=[
            pltpu.VMEM((2, 4, SUBS, LANES), f32),
            pltpu.SemaphoreType.DMA((2,)),
        ],
        input_output_aliases={0: 0},
        name="finish",
        cost_estimate=pl.CostEstimate(flops=1_000_000, bytes_accessed=400_000, transcendentals=0),
    )(
        interior,
        *(
            kept(array)
            for array in (
                edge,
                turned,
                fields,
                recv_a,
                recv_b,
                source,
                own,
                other,
                beyond,
                beyond_other,
                spin,
            )
        ),
    )
    return (next_state, densities, magnet_next)


def solution(mesh):
    return jax.shard_map(
        local,
        mesh=mesh,
        in_specs=(
            P(None, "modes", "sites"),
            P("sites"),
            P("sites"),
            P(None, "sites"),
            P("sites"),
            P("modes"),
            P(None, "modes"),
            P("modes"),
            P(),
            P("modes"),
        ),
        out_specs=(P(None, "modes", "sites"), P(None, "sites"), P(None, "sites")),
        check_vma=False,
    )
```

```python
import functools
import math

import jax
import jax.numpy as jnp
from jax import lax
from jax.experimental import pallas as pl
from jax.experimental.pallas import tpu as pltpu
from jax.sharding import PartitionSpec as P

time_step = 0.6
start_time = 10.0
exchange_coupling = 0.5
LANES = 128
SUBS = 8
PIECES = 4
STEP_COEF = (time_step / 4.0, time_step / 3.0, time_step / 2.0, time_step)
FIELDS_AT = 4 * SUBS
HEADS_AT = FIELDS_AT + SUBS
PACK_ROWS = HEADS_AT + SUBS


def lane_iota():
    return lax.broadcasted_iota(jnp.int32, (SUBS, LANES), 1)


def sub_iota():
    return lax.broadcasted_iota(jnp.int32, (SUBS, LANES), 0)


def shift_from_left(tile):
    return pltpu.roll(tile, 1, 1)


def shift_from_right(tile):
    return pltpu.roll(tile, LANES - 1, 1)


def column(read):
    rows = sub_iota()
    out = jnp.full((SUBS, LANES), read(0))
    for mode in range(1, SUBS):
        out = jnp.where(rows == mode, read(mode), out)
    return out


def source_terms(parts, masked_cos, masked_sin):
    up_real, down_real, up_imag, down_imag = parts
    return (
        masked_cos * up_real + masked_sin * down_real,
        masked_cos * down_real - masked_sin * up_real,
        masked_cos * up_imag + masked_sin * down_imag,
        masked_cos * down_imag - masked_sin * up_imag,
    )


def rotate_fore(state, cos_row, sin_row):
    return (
        cos_row * state[0] - sin_row * state[1],
        sin_row * state[0] + cos_row * state[1],
        cos_row * state[2] - sin_row * state[3],
        sin_row * state[2] + cos_row * state[3],
    )


def horner(base, state, hops, fields, source, coef):
    up_real, down_real, up_imag, down_imag = state
    plus, minus, field_x, field_y = fields
    h_up_real = plus * up_real + field_x * down_real + field_y * down_imag - hops[0] + source[0]
    h_down_real = minus * down_real + field_x * up_real - field_y * up_imag - hops[1] + source[1]
    h_up_imag = plus * up_imag + field_x * down_imag - field_y * down_real - hops[2] + source[2]
    h_down_imag = minus * down_imag + field_x * up_imag + field_y * up_real - hops[3] + source[3]
    return (
        base[0] + coef * h_up_imag,
        base[1] + coef * h_down_imag,
        base[2] - coef * h_up_real,
        base[3] - coef * h_down_real,
    )


def prepare_kernel(
    all_modes,
    wave_ref,
    potential_ref,
    angle_ref,
    magnet_ref,
    mask_ref,
    weight_ref,
    amp_ref,
    group_ref,
    energies_ref,
    lead_ref,
    turned_ref,
    fields_ref,
    payload_ref,
    pack_a_ref,
    pack_b_ref,
    tails_a_ref,
    tails_b_ref,
    source_ref,
    spin_ref,
    wave_in,
    sems,
):
    tiles = angle_ref.shape[0]
    piece = tiles * LANES // PIECES
    copies = [
        pltpu.make_async_copy(
            wave_ref.at[:, :, pl.ds(part * piece, piece)],
            wave_in.at[:, :, pl.ds(part * piece, piece)],
            sems.at[part],
        )
        for part in range(PIECES)
    ]
    for copy in copies:
        copy.start()

    lanes = lane_iota()
    site_index = lax.axis_index("sites")
    mode_index = lax.axis_index("modes")

    cosine = jnp.cos(angle_ref[...])
    sine = jnp.sin(angle_ref[...])
    fields_ref[4] = cosine
    fields_ref[5] = sine
    for part in range(3):
        for tile in range(tiles):
            spin_ref[part, tile : tile + 1, :] = magnet_ref[
                part : part + 1, tile * LANES : (tile + 1) * LANES
            ]
    mask = mask_ref[...].astype(jnp.float32)
    strength = exchange_coupling * mask
    field_x = strength * spin_ref[0]
    field_y = strength * spin_ref[1]
    field_z = strength * spin_ref[2]
    cos_two = cosine * cosine - sine * sine
    sin_two = 2.0 * (cosine * sine)
    turned_z = field_z * cos_two + field_x * sin_two
    fields_ref[0] = potential_ref[...] + turned_z
    fields_ref[1] = potential_ref[...] - turned_z
    fields_ref[2] = field_x * cos_two - field_z * sin_two
    fields_ref[3] = field_y
    spin_ref[3] = time_step * mask

    energy = column(lambda mode: energies_ref[group_ref[mode]])
    amps = [column(lambda mode, part=part: amp_ref[part, mode]) for part in range(4)]
    stages = []
    for offset in (0.0, 0.5 * time_step, time_step):
        phase = energy * (start_time + offset)
        cos_phase = jnp.cos(phase)
        sin_phase = jnp.sin(phase)
        stages.append(
            (
                amps[0] * cos_phase + amps[2] * sin_phase,
                amps[1] * cos_phase + amps[3] * sin_phase,
                amps[2] * cos_phase - amps[0] * sin_phase,
                amps[3] * cos_phase - amps[1] * sin_phase,
            )
        )
    first, middle, last = stages
    for part in range(4):
        combined = (
            first[part],
            0.5 * (first[part] + middle[part]),
            (first[part] + 2.0 * middle[part]) * (1.0 / 3.0),
            (first[part] + 4.0 * middle[part] + last[part]) * (1.0 / 6.0),
        )
        for step in range(4):
            source_ref[step * 4 + part] = combined[step]
    source_ref[16] = column(lambda mode: lead_ref[mode].astype(jnp.float32))

    weight = column(lambda mode: weight_ref[mode])
    charge_scale = 1.0 / all_modes
    spin_scale = 1.0 / math.sqrt(all_modes)
    nothing = (jnp.zeros((SUBS, LANES), jnp.float32),) * 4

    def rotated(tile):
        if tile == tiles:
            return nothing
        at = slice(tile * LANES, (tile + 1) * LANES)
        if tile * LANES % piece == 0:
            copies[tile * LANES // piece].wait()
        cos_row = fields_ref[4, tile : tile + 1, :]
        sin_row = fields_ref[5, tile : tile + 1, :]
        up_real, down_real, up_imag, down_imag = (wave_in[part, :, at] for part in range(4))
        out = (
            cos_row * up_real + sin_row * down_real,
            cos_row * down_real - sin_row * up_real,
            cos_row * up_imag + sin_row * down_imag,
            cos_row * down_imag - sin_row * up_imag,
        )
        for part in range(4):
            turned_ref[part, :, at] = out[part]
        return out

    here = rotated(0)
    here_rolled = [shift_from_right(x) for x in here]
    for tile in range(tiles):
        at = slice(tile * LANES, (tile + 1) * LANES)
        after = rotated(tile + 1)
        after_rolled = [shift_from_right(x) for x in after]
        up_real, down_real, up_imag, down_imag = (wave_in[part, :, at] for part in range(4))
        follow = [jnp.where(lanes == LANES - 1, b, a) for a, b in zip(here_rolled, after_rolled)]
        up_square = up_real * up_real + up_imag * up_imag
        down_square = down_real * down_real + down_imag * down_imag
        current = (
            here[0] * follow[2] + here[1] * follow[3] - here[2] * follow[0] - here[3] * follow[1]
        )
        rows = (
            (up_square + down_square, charge_scale),
            (up_real * down_real + up_imag * down_imag, 2.0 * spin_scale),
            (up_real * down_imag - up_imag * down_real, 2.0 * spin_scale),
            (up_square - down_square, spin_scale),
            (current, 2.0 * spin_scale),
        )
        for place, (value, scale) in enumerate(rows):
            payload_ref[place * tiles + tile : place * tiles + tile + 1, :] = scale * jnp.sum(
                value * weight, axis=0, keepdims=True
            )
        here, here_rolled = after, after_rolled

    slot = mode_index * 4
    scaled = (2.0 * spin_scale) * weight
    tails = jnp.zeros((SUBS, LANES), jnp.float32)
    heads = jnp.zeros((SUBS, LANES), jnp.float32)
    final = (tiles - 1) * LANES
    for part in range(4):
        tail_column = turned_ref[part, :, final + LANES - 1 : final + LANES]
        tails = jnp.where(lanes == slot + part, scaled * tail_column, tails)
        head_column = turned_ref[(part + 2) % 4, :, 0:1]
        head_column = head_column if part < 2 else -head_column
        heads = jnp.where(lanes == slot + part, head_column, heads)
    even = lax.rem(site_index, 2) == 0
    last = site_index == lax.axis_size("sites") - 1
    zero = jnp.zeros((SUBS, LANES), jnp.float32)
    tails_a_ref[...] = jnp.where(jnp.logical_and(even, jnp.logical_not(last)), tails, zero)
    tails_b_ref[...] = jnp.where(jnp.logical_or(even, last), zero, tails)

    for part in range(4):
        at = slice(part * SUBS, (part + 1) * SUBS)
        head = turned_ref[part, :, 0:LANES]
        tail = turned_ref[part, :, final : final + LANES]
        pack_a_ref[at, :] = jnp.where(even, tail, head)
        pack_b_ref[at, :] = jnp.where(even, head, tail)
    for place in range(6):
        at = slice(FIELDS_AT + place, FIELDS_AT + place + 1)
        head = fields_ref[place, 0:1, :]
        tail = fields_ref[place, tiles - 1 : tiles, :]
        pack_a_ref[at, :] = jnp.where(even, tail, head)
        pack_b_ref[at, :] = jnp.where(even, head, tail)
    for pack_ref in (pack_a_ref, pack_b_ref):
        pack_ref[FIELDS_AT + 6 : HEADS_AT, :] = jnp.zeros((2, LANES), jnp.float32)
        pack_ref[HEADS_AT:PACK_ROWS, :] = heads


def region_masks(positions, lead, span, cos_row, sin_row):
    offset = positions - lead
    inside = (offset >= 0.0) & (offset < span)
    zero = jnp.zeros((SUBS, LANES), jnp.float32)
    return jnp.where(inside, cos_row, zero), jnp.where(inside, sin_row, zero)


def advance_kernel(
    span, turned_ref, fields_ref, source_ref, recv_a_ref, recv_b_ref, next_ref, *scratch
):
    (work_a, work_b, out_ref, sems) = scratch
    tiles = fields_ref.shape[1]
    piece = tiles * LANES // PIECES
    lanes = lane_iota()
    site_index = lax.axis_index("sites")
    even = lax.rem(site_index, 2) == 0
    first_site = site_index * (tiles * LANES)
    lane_position = (lanes + first_site).astype(jnp.float32)
    lead = source_ref[16]
    zero = (jnp.zeros((SUBS, LANES), jnp.float32),) * 4
    targets = (work_a, work_b, work_a, out_ref)
    copies = [
        pltpu.make_async_copy(
            out_ref.at[:, :, pl.ds(part * piece, piece)],
            next_ref.at[:, :, pl.ds(part * piece, piece)],
            sems.at[part],
        )
        for part in range(PIECES)
    ]

    inside = {-1: site_index > 0, tiles: site_index < lax.axis_size("sites") - 1}
    halo = {}
    for tile, near, far in ((-1, recv_b_ref, recv_a_ref), (tiles, recv_a_ref, recv_b_ref)):
        base = tuple(
            jnp.where(
                inside[tile],
                jnp.where(
                    even,
                    near[part * SUBS : (part + 1) * SUBS, :],
                    far[part * SUBS : (part + 1) * SUBS, :],
                ),
                zero[0],
            )
            for part in range(4)
        )
        rows = [
            jnp.where(even, near[place : place + 1, :], far[place : place + 1, :])
            for place in range(FIELDS_AT, FIELDS_AT + 6)
        ]
        halo[tile] = (base, rows)
    halo_state = {tile: halo[tile][0] for tile in halo}

    for step in range(4):
        origin_ref = turned_ref if step == 0 else targets[step - 1]
        target_ref = targets[step]
        parts = [source_ref[step * 4 + part] for part in range(4)]
        next_halo = {}

        def load(tile):
            if tile in halo:
                return halo_state[tile]
            if tile > tiles:
                return zero
            return tuple(
                origin_ref[part, :, tile * LANES : (tile + 1) * LANES] for part in range(4)
            )

        before_up = zero
        here = load(-1)
        here_up = [shift_from_left(x) for x in here]
        here_down = [shift_from_right(x) for x in here]
        for tile in range(-1, tiles + 1):
            after = load(tile + 1)
            after_up = [shift_from_left(x) for x in after]
            after_down = [shift_from_right(x) for x in after]
            if tile not in halo or step < 3:
                if tile in halo:
                    base, rows = halo[tile]
                else:
                    at = slice(tile * LANES, (tile + 1) * LANES)
                    base = tuple(turned_ref[part, :, at] for part in range(4))
                    rows = [fields_ref[place, tile : tile + 1, :] for place in range(6)]
                hops = [
                    jnp.where(lanes == 0, b, a) + jnp.where(lanes == LANES - 1, d, c)
                    for a, b, c, d in zip(here_up, before_up, here_down, after_down)
                ]
                masked = region_masks(
                    lane_position + float(tile * LANES), lead, span, rows[4], rows[5]
                )
                out = horner(
                    base, here, hops, rows[:4], source_terms(parts, *masked), STEP_COEF[step]
                )
                if tile in halo:
                    next_halo[tile] = tuple(jnp.where(inside[tile], x, zero[0]) for x in out)
                else:
                    if step == 3:
                        out = rotate_fore(out, rows[4], rows[5])
                    for part in range(4):
                        target_ref[part, :, at] = out[part]
                    if step == 3 and (tile + 1) * LANES % piece == 0:
                        copies[tile * LANES // piece].start()
            before_up, here, here_up, here_down = here_up, after, after_up, after_down
        halo_state = next_halo

    for copy in copies:
        copy.wait()


def finish_kernel(
    own_ref, other_ref, corner_a_ref, corner_b_ref, spin_ref, densities_ref, magnet_next_ref
):
    tiles = spin_ref.shape[1]
    totals = []
    for place in range(5):
        rows = slice(place * tiles, (place + 1) * tiles)
        totals.append(own_ref[rows, :] + other_ref[rows, :])
    ends = slice(5 * tiles, 5 * tiles + SUBS)
    products = (own_ref[ends, :] + other_ref[ends, :]) + (corner_a_ref[...] + corner_b_ref[...])
    corner = jnp.sum(jnp.sum(products, axis=1, keepdims=True), axis=0, keepdims=True)
    row_at = lax.broadcasted_iota(jnp.int32, (tiles, LANES), 0)
    lane_at = lax.broadcasted_iota(jnp.int32, (tiles, LANES), 1)
    totals[4] = jnp.where((row_at == tiles - 1) & (lane_at == LANES - 1), corner, totals[4])
    for place in range(5):
        for tile in range(tiles):
            densities_ref[place : place + 1, tile * LANES : (tile + 1) * LANES] = totals[place][
                tile : tile + 1, :
            ]
    field_x, field_y, field_z = (exchange_coupling * totals[1 + part] for part in range(3))
    magnet_x, magnet_y, magnet_z = (spin_ref[part] for part in range(3))
    torque = (
        magnet_y * field_z - magnet_z * field_y,
        magnet_z * field_x - magnet_x * field_z,
        magnet_x * field_y - magnet_y * field_x,
    )
    for part, magnet in enumerate((magnet_x, magnet_y, magnet_z)):
        advanced = magnet - spin_ref[3] * torque[part]
        for tile in range(tiles):
            magnet_next_ref[part : part + 1, tile * LANES : (tile + 1) * LANES] = advanced[
                tile : tile + 1, :
            ]


def local(
    wave_state,
    potential,
    spin_angle,
    magnet,
    magnetic_mask,
    mode_weight,
    source_amp,
    mode_group,
    energies,
    lead_site,
):
    local_modes, local_sites = wave_state.shape[1:]
    site_count = lax.axis_size("sites")
    mode_count = lax.axis_size("modes")
    assert local_modes == SUBS and local_sites % (LANES * PIECES) == 0
    tiles = local_sites // LANES
    span = float(local_sites * site_count // 8)
    f32 = jnp.float32
    vmem = pl.BlockSpec(memory_space=pltpu.VMEM)
    smem = pl.BlockSpec(memory_space=pltpu.SMEM)
    anywhere = pl.BlockSpec(memory_space=pl.ANY)
    dense = (tiles, LANES)
    kept = lambda array: pltpu.with_memory_space_constraint(array, pltpu.VMEM)

    turned, fields, payload, pack_a, pack_b, tails_a, tails_b, source, spin = pl.pallas_call(
        functools.partial(prepare_kernel, local_modes * mode_count),
        out_shape=(
            pltpu.VMEM(wave_state.shape, f32),
            pltpu.VMEM((6,) + dense, f32),
            pltpu.VMEM((5 * tiles, LANES), f32),
            pltpu.VMEM((PACK_ROWS, LANES), f32),
            pltpu.VMEM((PACK_ROWS, LANES), f32),
            pltpu.VMEM((SUBS, LANES), f32),
            pltpu.VMEM((SUBS, LANES), f32),
            pltpu.VMEM((17, SUBS, LANES), f32),
            pltpu.VMEM((4,) + dense, f32),
        ),
        in_specs=[anywhere] + [vmem] * 4 + [smem] * 5,
        out_specs=[vmem] * 9,
        scratch_shapes=[
            pltpu.VMEM(wave_state.shape, f32),
            pltpu.SemaphoreType.DMA((PIECES,)),
        ],
        name="prepare",
        cost_estimate=pl.CostEstimate(flops=10_000_000, bytes_accessed=1_500_000, transcendentals=0),
    )(
        wave_state,
        potential.reshape(dense),
        spin_angle.reshape(dense),
        magnet,
        magnetic_mask.reshape(dense),
        mode_weight,
        source_amp,
        mode_group,
        energies,
        lead_site,
    )

    def swap_sites(pack, pairs):
        partner = {i: j for pair in pairs for i, j in (pair, pair[::-1])}
        whole = [
            (
                m * site_count + s,
                m * site_count + partner[s] if s in partner else (m ^ 1) * site_count + s,
            )
            for m in range(mode_count)
            for s in range(site_count)
        ]
        return lax.ppermute(pack, ("modes", "sites"), whole)

    def swap_modes(array, distance):
        return lax.ppermute(array, "modes", [(i, i ^ distance) for i in range(mode_count)])

    recv_b = swap_sites(pack_b, [(i, i + 1) for i in range(1, site_count - 1, 2)])
    recv_a = swap_sites(pack_a, [(i, i + 1) for i in range(0, site_count - 1, 2)])
    product = tails_a * recv_a[HEADS_AT:] + tails_b * recv_b[HEADS_AT:]

    if mode_count == 4:
        own = payload + swap_modes(payload, 1)
        own = jnp.concatenate([own, product])
        other = swap_modes(own, 2)
        corner_a = swap_modes(product, 3)
        corner_b = swap_modes(product, 1)
    else:
        own = jnp.concatenate([payload, product])
        distance = 1
        while 2 * distance < mode_count:
            own = own + swap_modes(own, distance)
            distance *= 2
        other = swap_modes(own, distance)
        corner_a = corner_b = jnp.zeros_like(product)

    next_state = pl.pallas_call(
        functools.partial(advance_kernel, span),
        out_shape=jax.ShapeDtypeStruct(wave_state.shape, f32),
        in_specs=[vmem] * 5,
        out_specs=anywhere,
        scratch_shapes=[pltpu.VMEM(wave_state.shape, f32)] * 3
        + [pltpu.SemaphoreType.DMA((PIECES,))],
        name="advance",
        cost_estimate=pl.CostEstimate(flops=20_000_000, bytes_accessed=1_500_000, transcendentals=0),
    )(kept(turned), kept(fields), kept(source), kept(recv_a), kept(recv_b))

    densities, magnet_next = pl.pallas_call(
        finish_kernel,
        out_shape=(
            jax.ShapeDtypeStruct((5, local_sites), f32),
            jax.ShapeDtypeStruct((3, local_sites), f32),
        ),
        in_specs=[vmem] * 5,
        out_specs=[vmem, vmem],
        name="finish",
        cost_estimate=pl.CostEstimate(flops=1_000_000, bytes_accessed=400_000, transcendentals=0),
    )(kept(own), kept(other), kept(corner_a), kept(corner_b), kept(spin))
    return (next_state, densities, magnet_next)


def solution(mesh):
    return jax.shard_map(
        local,
        mesh=mesh,
        in_specs=(
            P(None, "modes", "sites"),
            P("sites"),
            P("sites"),
            P(None, "sites"),
            P("sites"),
            P("modes"),
            P(None, "modes"),
            P("modes"),
            P(),
            P("modes"),
        ),
        out_specs=(P(None, "modes", "sites"), P(None, "sites"), P(None, "sites")),
        check_vma=False,
    )
```

```python
import functools
import math

import jax
import jax.numpy as jnp
from jax import lax
from jax.experimental import pallas as pl
from jax.experimental.pallas import tpu as pltpu
from jax.sharding import PartitionSpec as P

time_step = 0.6
start_time = 10.0
exchange_coupling = 0.5
LANES = 128
SUBS = 8
PIECES = 4
STEP_COEF = (time_step / 4.0, time_step / 3.0, time_step / 2.0, time_step)
REACH = 4


def lane_iota():
    return lax.broadcasted_iota(jnp.int32, (SUBS, LANES), 1)


def sub_iota():
    return lax.broadcasted_iota(jnp.int32, (SUBS, LANES), 0)


def shift_from_left(tile):
    return pltpu.roll(tile, 1, 1)


def shift_from_right(tile):
    return pltpu.roll(tile, LANES - 1, 1)


def column(row):
    count = row.shape[1]
    shape = (count, count)
    same = lax.broadcasted_iota(jnp.int32, shape, 0) == lax.broadcasted_iota(jnp.int32, shape, 1)
    spread = jnp.broadcast_to(row, shape)
    return jnp.sum(jnp.where(same, spread, jnp.zeros_like(spread)), axis=1, keepdims=True)


def source_terms(parts, masked_cos, masked_sin):
    up_real, down_real, up_imag, down_imag = parts
    return (
        masked_cos * up_real + masked_sin * down_real,
        masked_cos * down_real - masked_sin * up_real,
        masked_cos * up_imag + masked_sin * down_imag,
        masked_cos * down_imag - masked_sin * up_imag,
    )


def rotate_fore(state, cos_row, sin_row):
    return (
        cos_row * state[0] - sin_row * state[1],
        sin_row * state[0] + cos_row * state[1],
        cos_row * state[2] - sin_row * state[3],
        sin_row * state[2] + cos_row * state[3],
    )


def rotate_back(state, cos_row, sin_row):
    return (
        cos_row * state[0] + sin_row * state[1],
        cos_row * state[1] - sin_row * state[0],
        cos_row * state[2] + sin_row * state[3],
        cos_row * state[3] - sin_row * state[2],
    )


def horner(base, state, hops, fields, source, coef):
    up_real, down_real, up_imag, down_imag = state
    plus, minus, field_x, field_y = fields
    h_up_real = plus * up_real + field_x * down_real + field_y * down_imag - hops[0] + source[0]
    h_down_real = minus * down_real + field_x * up_real - field_y * up_imag - hops[1] + source[1]
    h_up_imag = plus * up_imag + field_x * down_imag - field_y * down_real - hops[2] + source[2]
    h_down_imag = minus * down_imag + field_x * up_imag + field_y * up_real - hops[3] + source[3]
    return (
        base[0] + coef * h_up_imag,
        base[1] + coef * h_down_imag,
        base[2] - coef * h_up_real,
        base[3] - coef * h_down_real,
    )


def field_rows(potential, cosine, sine, field):
    field_x, field_y, field_z = field
    cos_two = cosine * cosine - sine * sine
    sin_two = 2.0 * (cosine * sine)
    turned_z = field_z * cos_two + field_x * sin_two
    return (
        potential + turned_z,
        potential - turned_z,
        field_x * cos_two - field_z * sin_two,
        field_y,
    )


def edge_kernel(
    wave_ref,
    potential_ref,
    angle_ref,
    magnet_ref,
    mask_ref,
    weight_ref,
    amp_ref,
    group_ref,
    energies_ref,
    lead_ref,
    pack_a_ref,
    pack_b_ref,
    tails_a_ref,
    tails_b_ref,
    weight_out_ref,
    potential_in,
    magnet_in,
    mask_in,
    amp_in,
    group_in,
    energies_in,
    lead_in,
    angle_in,
    edge_in,
    weight_in,
    sems,
):
    tiles = angle_ref.shape[0]
    final = (tiles - 1) * LANES
    moves = [
        (wave_ref.at[:, :, pl.ds(side * final, LANES)], edge_in.at[side]) for side in range(2)
    ]
    moves += [
        (angle_ref, angle_in),
        (mask_ref, mask_in),
        (magnet_ref, magnet_in),
        (potential_ref, potential_in),
    ]
    moves += [(weight_ref, weight_in)]
    moves += [
        (amp_ref, amp_in),
        (group_ref, group_in),
        (energies_ref, energies_in),
        (lead_ref, lead_in),
    ]
    moving = [
        pltpu.make_async_copy(source, target, sems.at[place])
        for place, (source, target) in enumerate(moves)
    ]
    for copy in moving:
        copy.start()
    lanes = lane_iota()
    site_index = lax.axis_index("sites")
    even = lax.rem(site_index, 2) == 0
    last = site_index == lax.axis_size("sites") - 1
    zero = jnp.zeros((SUBS, LANES), jnp.float32)
    for copy in moving[:7]:
        copy.wait()
    weight = jnp.broadcast_to(column(weight_in[...]), (SUBS, LANES))
    weight_out_ref[...] = weight

    turned = []
    fields = []
    for side, row in ((0, 0), (1, tiles - 1)):
        at = slice(row * LANES, (row + 1) * LANES)
        cosine = jnp.cos(angle_in[row : row + 1, :])
        sine = jnp.sin(angle_in[row : row + 1, :])
        strength = exchange_coupling * mask_in[row : row + 1, :].astype(jnp.float32)
        field = [strength * magnet_in[part : part + 1, at] for part in range(3)]
        potential = potential_in[row : row + 1, :]
        fields.append(field_rows(potential, cosine, sine, field) + (cosine, sine))
        turned.append(rotate_back([edge_in[side, part] for part in range(4)], cosine, sine))
    head, tail = turned

    tails = zero
    for part in range(4):
        end = tail[(part + 2) % 4][:, LANES - 1 : LANES]
        tails = jnp.where(lanes == REACH * part, -end if part < 2 else end, tails)
    tails_a_ref[...] = jnp.where(jnp.logical_and(even, jnp.logical_not(last)), tails, zero)
    tails_b_ref[...] = jnp.where(jnp.logical_or(even, last), zero, tails)

    rows = sub_iota()
    packs = []
    for side in range(2):
        blocks = list(turned[side])
        block = jnp.broadcast_to(fields[side][0], (SUBS, LANES))
        for place in range(1, 6):
            block = jnp.where(rows == place, fields[side][place], block)
        blocks.append(block)
        pack = zero
        for part, block in enumerate(blocks):
            shift = REACH * (part + side) % LANES
            moved = pltpu.roll(block, shift, 1) if shift else block
            pack = jnp.where(lanes // REACH == part, moved, pack)
        packs.append(pack)
    pack_a_ref[...] = jnp.where(even, packs[1], packs[0])
    pack_b_ref[...] = jnp.where(even, packs[0], packs[1])

    for copy in moving[7:]:
        copy.wait()


def density_kernel(all_modes, wave_ref, angle_ref, weight_ref, turned_ref, trig_ref, payload_ref):
    tiles = angle_ref.shape[0]
    lanes = lane_iota()
    trig_ref[0] = jnp.cos(angle_ref[...])
    trig_ref[1] = jnp.sin(angle_ref[...])

    weight = weight_ref[...]
    charge_scale = 1.0 / all_modes
    spin_scale = 1.0 / math.sqrt(all_modes)
    nothing = (jnp.zeros((SUBS, LANES), jnp.float32),) * 4

    def rotated(tile):
        if tile == tiles:
            return nothing
        at = slice(tile * LANES, (tile + 1) * LANES)
        cos_row = trig_ref[0, tile : tile + 1, :]
        sin_row = trig_ref[1, tile : tile + 1, :]
        out = rotate_back([wave_ref[part, :, at] for part in range(4)], cos_row, sin_row)
        for part in range(4):
            turned_ref[part, :, at] = out[part]
        return out

    here = rotated(0)
    here_rolled = [shift_from_right(x) for x in here]
    for tile in range(tiles):
        at = slice(tile * LANES, (tile + 1) * LANES)
        after = rotated(tile + 1)
        after_rolled = [shift_from_right(x) for x in after]
        up_real, down_real, up_imag, down_imag = (wave_ref[part, :, at] for part in range(4))
        follow = [jnp.where(lanes == LANES - 1, b, a) for a, b in zip(here_rolled, after_rolled)]
        up_square = up_real * up_real + up_imag * up_imag
        down_square = down_real * down_real + down_imag * down_imag
        current = (
            here[0] * follow[2] + here[1] * follow[3] - here[2] * follow[0] - here[3] * follow[1]
        )
        rows = (
            (up_square + down_square, charge_scale),
            (up_real * down_real + up_imag * down_imag, 2.0 * spin_scale),
            (up_real * down_imag - up_imag * down_real, 2.0 * spin_scale),
            (up_square - down_square, spin_scale),
            (current, 2.0 * spin_scale),
        )
        for place, (value, scale) in enumerate(rows):
            payload_ref[place * tiles + tile : place * tiles + tile + 1, :] = scale * jnp.sum(
                value * weight, axis=0, keepdims=True
            )
        here, here_rolled = after, after_rolled


def region_masks(positions, lead, span, cos_row, sin_row):
    offset = positions - lead
    inside = (offset >= 0.0) & (offset < span)
    zero = jnp.zeros((SUBS, LANES), jnp.float32)
    return jnp.where(inside, cos_row, zero), jnp.where(inside, sin_row, zero)


def setup_kernel(
    scale,
    weight_ref,
    trig_ref,
    potential_ref,
    magnet_ref,
    mask_ref,
    amp_ref,
    group_ref,
    energies_ref,
    lead_ref,
    fields_ref,
    source_ref,
    spin_ref,
    scaled_ref,
):
    tiles = trig_ref.shape[1]
    scaled_ref[...] = scale * weight_ref[...]
    cosine = trig_ref[0]
    sine = trig_ref[1]
    for part in range(3):
        for tile in range(tiles):
            spin_ref[part, tile : tile + 1, :] = magnet_ref[
                part : part + 1, tile * LANES : (tile + 1) * LANES
            ]
    mask = mask_ref[...].astype(jnp.float32)
    strength = exchange_coupling * mask
    field = [strength * spin_ref[part] for part in range(3)]
    for place, value in enumerate(field_rows(potential_ref[...], cosine, sine, field)):
        fields_ref[place] = value
    spin_ref[3] = time_step * mask

    table = (SUBS, energies_ref.shape[1])
    chosen = column(group_ref[...].astype(jnp.float32)) == lax.broadcasted_iota(
        jnp.int32, table, 1
    ).astype(jnp.float32)
    values = jnp.broadcast_to(energies_ref[...], table)
    energy = jnp.sum(jnp.where(chosen, values, jnp.zeros_like(values)), axis=1, keepdims=True)
    energy = jnp.broadcast_to(energy, (SUBS, LANES))
    amps = [
        jnp.broadcast_to(column(amp_ref[part : part + 1, :]), (SUBS, LANES)) for part in range(4)
    ]
    stages = []
    for offset in (0.0, 0.5 * time_step, time_step):
        phase = energy * (start_time + offset)
        cos_phase = jnp.cos(phase)
        sin_phase = jnp.sin(phase)
        stages.append(
            (
                amps[0] * cos_phase + amps[2] * sin_phase,
                amps[1] * cos_phase + amps[3] * sin_phase,
                amps[2] * cos_phase - amps[0] * sin_phase,
                amps[3] * cos_phase - amps[1] * sin_phase,
            )
        )
    first, middle, last = stages
    for part in range(4):
        combined = (
            first[part],
            0.5 * (first[part] + middle[part]),
            (first[part] + 2.0 * middle[part]) * (1.0 / 3.0),
            (first[part] + 4.0 * middle[part] + last[part]) * (1.0 / 6.0),
        )
        for step in range(4):
            source_ref[step * 4 + part] = combined[step]
    source_ref[16] = jnp.broadcast_to(column(lead_ref[...].astype(jnp.float32)), (SUBS, LANES))


def advance_kernel(
    span,
    turned_ref,
    trig_ref,
    recv_b_ref,
    recv_a_ref,
    fields_ref,
    source_ref,
    next_ref,
    out_ref,
    work_a,
    work_b,
    sem,
):
    tiles = trig_ref.shape[1]
    piece = tiles * LANES // PIECES
    lanes = lane_iota()
    site_index = lax.axis_index("sites")
    even = lax.rem(site_index, 2) == 0
    first_site = site_index * (tiles * LANES)
    lane_position = (lanes + first_site).astype(jnp.float32)
    lead = source_ref[16]
    zero = (jnp.zeros((SUBS, LANES), jnp.float32),) * 4
    targets = (work_a, work_b, work_a, out_ref)
    copy = pltpu.make_async_copy(
        out_ref.at[:, :, pl.ds(0, piece)], next_ref.at[:, :, pl.ds(0, piece)], sem
    )

    inside = {-1: site_index > 0, tiles: site_index < lax.axis_size("sites") - 1}
    halo = {}
    for tile, near_ref, far_ref in ((-1, recv_b_ref, recv_a_ref), (tiles, recv_a_ref, recv_b_ref)):
        pack = jnp.where(even, near_ref[...], far_ref[...])
        pack = jnp.where(inside[tile], pack, zero[0])
        start = LANES - REACH if tile < 0 else 0
        blocks = []
        for part in range(5):
            shift = (start - REACH * part) % LANES
            blocks.append(pltpu.roll(pack, shift, 1) if shift else pack)
        halo[tile] = (tuple(blocks[:4]), [blocks[4][place : place + 1, :] for place in range(6)])
    halo_state = {tile: halo[tile][0] for tile in halo}

    for step in range(4):
        origin_ref = turned_ref if step == 0 else targets[step - 1]
        target_ref = targets[step]
        parts = [source_ref[step * 4 + part] for part in range(4)]
        next_halo = {}

        def load(tile):
            if tile in halo:
                return halo_state[tile]
            if tile > tiles:
                return zero
            return tuple(
                origin_ref[part, :, tile * LANES : (tile + 1) * LANES] for part in range(4)
            )

        before_up = zero
        here = load(-1)
        here_up = [shift_from_left(x) for x in here]
        here_down = [shift_from_right(x) for x in here]
        for tile in range(-1, tiles + 1):
            after = load(tile + 1)
            after_up = [shift_from_left(x) for x in after]
            after_down = [shift_from_right(x) for x in after]
            if tile not in halo or step < 3:
                if tile in halo:
                    base, rows = halo[tile]
                else:
                    at = slice(tile * LANES, (tile + 1) * LANES)
                    base = tuple(turned_ref[part, :, at] for part in range(4))
                    rows = [fields_ref[place, tile : tile + 1, :] for place in range(4)]
                    rows += [trig_ref[place, tile : tile + 1, :] for place in range(2)]
                hops = [
                    jnp.where(lanes == 0, b, a) + jnp.where(lanes == LANES - 1, d, c)
                    for a, b, c, d in zip(here_up, before_up, here_down, after_down)
                ]
                masked = region_masks(
                    lane_position + float(tile * LANES), lead, span, rows[4], rows[5]
                )
                out = horner(
                    base, here, hops, rows[:4], source_terms(parts, *masked), STEP_COEF[step]
                )
                if tile in halo:
                    next_halo[tile] = tuple(jnp.where(inside[tile], x, zero[0]) for x in out)
                else:
                    if step == 3:
                        out = rotate_fore(out, rows[4], rows[5])
                    for part in range(4):
                        target_ref[part, :, at] = out[part]
                    if step == 3 and (tile + 1) * LANES == piece:
                        copy.start()
            before_up, here, here_up, here_down = here_up, after, after_up, after_down
        halo_state = next_halo

    copy.wait()


def finish_kernel(
    next_in_ref,
    out_ref,
    own_ref,
    other_ref,
    corner_ref,
    corner_other_ref,
    spin_ref,
    next_ref,
    densities_ref,
    magnet_next_ref,
    densities_out,
    magnet_out,
    sems,
):
    tiles = spin_ref.shape[1]
    piece = tiles * LANES // PIECES
    rest = pl.ds(piece, tiles * LANES - piece)
    copies = [
        pltpu.make_async_copy(out_ref.at[:, :, rest], next_ref.at[:, :, rest], sems.at[0]),
        pltpu.make_async_copy(densities_out, densities_ref, sems.at[1]),
        pltpu.make_async_copy(magnet_out, magnet_next_ref, sems.at[2]),
    ]
    copies[0].start()
    totals = []
    for place in range(5):
        rows = slice(place * tiles, (place + 1) * tiles)
        totals.append(own_ref[rows, :] + other_ref[rows, :])
    products = corner_ref[...] + corner_other_ref[...]
    corner = jnp.sum(jnp.sum(products, axis=1, keepdims=True), axis=0, keepdims=True)
    row_at = lax.broadcasted_iota(jnp.int32, (tiles, LANES), 0)
    lane_at = lax.broadcasted_iota(jnp.int32, (tiles, LANES), 1)
    totals[4] = jnp.where((row_at == tiles - 1) & (lane_at == LANES - 1), corner, totals[4])
    for place in range(5):
        for tile in range(tiles):
            densities_out[place : place + 1, tile * LANES : (tile + 1) * LANES] = totals[place][
                tile : tile + 1, :
            ]
    copies[1].start()
    field_x, field_y, field_z = (exchange_coupling * totals[1 + part] for part in range(3))
    magnet_x, magnet_y, magnet_z = (spin_ref[part] for part in range(3))
    torque = (
        magnet_y * field_z - magnet_z * field_y,
        magnet_z * field_x - magnet_x * field_z,
        magnet_x * field_y - magnet_y * field_x,
    )
    for part, magnet in enumerate((magnet_x, magnet_y, magnet_z)):
        advanced = magnet - spin_ref[3] * torque[part]
        for tile in range(tiles):
            magnet_out[part : part + 1, tile * LANES : (tile + 1) * LANES] = advanced[
                tile : tile + 1, :
            ]
    copies[2].start()
    for copy in copies:
        copy.wait()


def local(
    wave_state,
    potential,
    spin_angle,
    magnet,
    magnetic_mask,
    mode_weight,
    source_amp,
    mode_group,
    energies,
    lead_site,
):
    local_modes, local_sites = wave_state.shape[1:]
    site_count = lax.axis_size("sites")
    mode_count = lax.axis_size("modes")
    assert local_modes == SUBS and local_sites % (LANES * PIECES) == 0
    tiles = local_sites // LANES
    span = float(local_sites * site_count // 8)
    f32 = jnp.float32
    vmem = pl.BlockSpec(memory_space=pltpu.VMEM)
    anywhere = pl.BlockSpec(memory_space=pl.ANY)
    dense = (tiles, LANES)
    kept = lambda array: pltpu.with_memory_space_constraint(array, pltpu.VMEM)

    potential = potential.reshape(dense)
    spin_angle = spin_angle.reshape(dense)
    magnetic_mask = magnetic_mask.reshape(dense)

    row = lambda array: array.reshape(1, -1)
    small = (row(mode_weight), source_amp, row(mode_group), row(energies), row(lead_site))
    site_arrays = (potential, magnet, magnetic_mask)
    (pack_a, pack_b, tails_a, tails_b, weight, *staged, angle_staged) = pl.pallas_call(
        edge_kernel,
        out_shape=(
            *(pltpu.VMEM((SUBS, LANES), f32) for _ in range(5)),
            *(pltpu.VMEM(array.shape, array.dtype) for array in site_arrays + small[1:]),
            pltpu.VMEM(dense, f32),
        ),
        in_specs=[anywhere] * 10,
        out_specs=[vmem] * 13,
        scratch_shapes=[
            pltpu.VMEM((2, 4, SUBS, LANES), f32),
            pltpu.VMEM(small[0].shape, f32),
            pltpu.SemaphoreType.DMA((11,)),
        ],
        name="edges",
        cost_estimate=pl.CostEstimate(flops=100_000, bytes_accessed=200_000, transcendentals=0),
    )(wave_state, potential, spin_angle, magnet, magnetic_mask, *small)

    wave_late, pack_b = lax.optimization_barrier((wave_state, pack_b))
    turned, trig, payload = pl.pallas_call(
        functools.partial(density_kernel, local_modes * mode_count),
        out_shape=(
            pltpu.VMEM(wave_state.shape, f32),
            pltpu.VMEM((2,) + dense, f32),
            pltpu.VMEM((5 * tiles, LANES), f32),
        ),
        in_specs=[vmem] * 3,
        out_specs=[vmem] * 3,
        name="densities",
        cost_estimate=pl.CostEstimate(flops=10_000_000, bytes_accessed=1_500_000, transcendentals=0),
    )(kept(wave_late), kept(angle_staged), kept(weight))
    payload, pack_a = lax.optimization_barrier((payload, pack_a))

    def swap_sites(pack, pairs):
        partner = {i: j for pair in pairs for i, j in (pair, pair[::-1])}
        whole = [
            (
                m * site_count + s,
                m * site_count + partner[s] if s in partner else (m ^ 1) * site_count + s,
            )
            for m in range(mode_count)
            for s in range(site_count)
        ]
        return lax.ppermute(pack, ("modes", "sites"), whole)

    def swap_modes(array, distance):
        return lax.ppermute(array, "modes", [(i, i ^ distance) for i in range(mode_count)])

    recv_b = swap_sites(pack_b, [(i, i + 1) for i in range(1, site_count - 1, 2)])
    recv_a = swap_sites(pack_a, [(i, i + 1) for i in range(0, site_count - 1, 2)])
    distance = 1
    while 2 * distance < mode_count:
        payload = payload + swap_modes(payload, distance)
        distance *= 2
    last_distance = distance + 1 if distance > 1 else distance
    payload, weight = lax.optimization_barrier((payload, weight))
    payload_other = swap_modes(payload, last_distance)

    fields, source, spin, scaled = pl.pallas_call(
        functools.partial(setup_kernel, 2.0 / math.sqrt(local_modes * mode_count)),
        out_shape=(
            pltpu.VMEM((4,) + dense, f32),
            pltpu.VMEM((17, SUBS, LANES), f32),
            pltpu.VMEM((4,) + dense, f32),
            pltpu.VMEM((SUBS, LANES), f32),
        ),
        in_specs=[vmem] * 9,
        out_specs=[vmem] * 4,
        name="setup",
        cost_estimate=pl.CostEstimate(flops=1_000_000, bytes_accessed=200_000, transcendentals=0),
    )(kept(weight), kept(trig), *(kept(array) for array in staged))

    product = scaled * (tails_b * recv_b + tails_a * recv_a)
    distance = 1
    while 2 * distance < mode_count:
        product = product + swap_modes(product, distance)
        distance *= 2
    product_other = swap_modes(product, last_distance)


    next_state, advanced = pl.pallas_call(
        functools.partial(advance_kernel, span),
        out_shape=(
            jax.ShapeDtypeStruct(wave_state.shape, f32),
            pltpu.VMEM(wave_state.shape, f32),
        ),
        in_specs=[vmem] * 6,
        out_specs=[anywhere, vmem],
        scratch_shapes=[pltpu.VMEM(wave_state.shape, f32)] * 2 + [pltpu.SemaphoreType.DMA],
        name="advance",
        cost_estimate=pl.CostEstimate(flops=20_000_000, bytes_accessed=1_500_000, transcendentals=0),
    )(kept(turned), kept(trig), kept(recv_b), kept(recv_a), kept(fields), kept(source))

    return pl.pallas_call(
        finish_kernel,
        out_shape=(
            jax.ShapeDtypeStruct(wave_state.shape, f32),
            jax.ShapeDtypeStruct((5, local_sites), f32),
            jax.ShapeDtypeStruct((3, local_sites), f32),
        ),
        in_specs=[anywhere] + [vmem] * 6,
        out_specs=[anywhere] * 3,
        scratch_shapes=[
            pltpu.VMEM((5, local_sites), f32),
            pltpu.VMEM((3, local_sites), f32),
            pltpu.SemaphoreType.DMA((3,)),
        ],
        input_output_aliases={0: 0},
        name="finish",
        cost_estimate=pl.CostEstimate(flops=1_000_000, bytes_accessed=400_000, transcendentals=0),
    )(
        next_state,
        kept(advanced),
        kept(payload),
        kept(payload_other),
        kept(product),
        kept(product_other),
        kept(spin),
    )


def solution(mesh):
    return jax.shard_map(
        local,
        mesh=mesh,
        in_specs=(
            P(None, "modes", "sites"),
            P("sites"),
            P("sites"),
            P(None, "sites"),
            P("sites"),
            P("modes"),
            P(None, "modes"),
            P("modes"),
            P(),
            P("modes"),
        ),
        out_specs=(P(None, "modes", "sites"), P(None, "sites"), P(None, "sites")),
        check_vma=False,
    )
```

```python
import functools
import math

import jax
import jax.numpy as jnp
from jax import lax
from jax.experimental import pallas as pl
from jax.experimental.pallas import tpu as pltpu
from jax.sharding import PartitionSpec as P

time_step = 0.6
start_time = 10.0
exchange_coupling = 0.5
LANES = 128
SUBS = 8
PIECES = 4
STEP_COEF = (time_step / 4.0, time_step / 3.0, time_step / 2.0, time_step)
REACH = 4


def lane_iota():
    return lax.broadcasted_iota(jnp.int32, (SUBS, LANES), 1)


def sub_iota():
    return lax.broadcasted_iota(jnp.int32, (SUBS, LANES), 0)


def shift_from_left(tile):
    return pltpu.roll(tile, 1, 1)


def shift_from_right(tile):
    return pltpu.roll(tile, LANES - 1, 1)


def column(row):
    count = row.shape[1]
    shape = (count, count)
    same = lax.broadcasted_iota(jnp.int32, shape, 0) == lax.broadcasted_iota(jnp.int32, shape, 1)
    spread = jnp.broadcast_to(row, shape)
    return jnp.sum(jnp.where(same, spread, jnp.zeros_like(spread)), axis=1, keepdims=True)


def source_terms(parts, masked_cos, masked_sin):
    up_real, down_real, up_imag, down_imag = parts
    return (
        masked_cos * up_real + masked_sin * down_real,
        masked_cos * down_real - masked_sin * up_real,
        masked_cos * up_imag + masked_sin * down_imag,
        masked_cos * down_imag - masked_sin * up_imag,
    )


def rotate_fore(state, cos_row, sin_row):
    return (
        cos_row * state[0] - sin_row * state[1],
        sin_row * state[0] + cos_row * state[1],
        cos_row * state[2] - sin_row * state[3],
        sin_row * state[2] + cos_row * state[3],
    )


def rotate_back(state, cos_row, sin_row):
    return (
        cos_row * state[0] + sin_row * state[1],
        cos_row * state[1] - sin_row * state[0],
        cos_row * state[2] + sin_row * state[3],
        cos_row * state[3] - sin_row * state[2],
    )


def horner(base, state, hops, fields, source, coef):
    up_real, down_real, up_imag, down_imag = state
    plus, minus, field_x, field_y = fields
    h_up_real = plus * up_real + field_x * down_real + field_y * down_imag - hops[0] + source[0]
    h_down_real = minus * down_real + field_x * up_real - field_y * up_imag - hops[1] + source[1]
    h_up_imag = plus * up_imag + field_x * down_imag - field_y * down_real - hops[2] + source[2]
    h_down_imag = minus * down_imag + field_x * up_imag + field_y * up_real - hops[3] + source[3]
    return (
        base[0] + coef * h_up_imag,
        base[1] + coef * h_down_imag,
        base[2] - coef * h_up_real,
        base[3] - coef * h_down_real,
    )


def field_rows(potential, cosine, sine, field):
    field_x, field_y, field_z = field
    cos_two = cosine * cosine - sine * sine
    sin_two = 2.0 * (cosine * sine)
    turned_z = field_z * cos_two + field_x * sin_two
    return (
        potential + turned_z,
        potential - turned_z,
        field_x * cos_two - field_z * sin_two,
        field_y,
    )


def edge_kernel(
    wave_ref,
    potential_ref,
    angle_ref,
    magnet_ref,
    mask_ref,
    weight_ref,
    amp_ref,
    group_ref,
    energies_ref,
    lead_ref,
    pack_a_ref,
    pack_b_ref,
    tails_first_ref,
    tails_a_ref,
    tails_b_ref,
    weight_out_ref,
    potential_in,
    magnet_in,
    mask_in,
    amp_in,
    group_in,
    energies_in,
    lead_in,
    angle_in,
    edge_in,
    weight_in,
    sems,
):
    tiles = angle_ref.shape[0]
    final = (tiles - 1) * LANES
    moves = [
        (wave_ref.at[:, :, pl.ds(side * final, LANES)], edge_in.at[side]) for side in range(2)
    ]
    moves += [
        (angle_ref, angle_in),
        (mask_ref, mask_in),
        (magnet_ref, magnet_in),
        (potential_ref, potential_in),
    ]
    moves += [(weight_ref, weight_in)]
    moves += [
        (amp_ref, amp_in),
        (group_ref, group_in),
        (energies_ref, energies_in),
        (lead_ref, lead_in),
    ]
    moving = [
        pltpu.make_async_copy(source, target, sems.at[place])
        for place, (source, target) in enumerate(moves)
    ]
    for copy in moving:
        copy.start()
    lanes = lane_iota()
    site_index = lax.axis_index("sites")
    even = lax.rem(site_index, 2) == 0
    first = site_index == 0
    last = site_index == lax.axis_size("sites") - 1
    zero = jnp.zeros((SUBS, LANES), jnp.float32)
    for copy in moving[:7]:
        copy.wait()
    weight = jnp.broadcast_to(column(weight_in[...]), (SUBS, LANES))
    weight_out_ref[...] = weight

    turned = []
    fields = []
    for side, row in ((0, 0), (1, tiles - 1)):
        at = slice(row * LANES, (row + 1) * LANES)
        cosine = jnp.cos(angle_in[row : row + 1, :])
        sine = jnp.sin(angle_in[row : row + 1, :])
        strength = exchange_coupling * mask_in[row : row + 1, :].astype(jnp.float32)
        field = [strength * magnet_in[part : part + 1, at] for part in range(3)]
        potential = potential_in[row : row + 1, :]
        fields.append(field_rows(potential, cosine, sine, field) + (cosine, sine))
        turned.append(rotate_back([edge_in[side, part] for part in range(4)], cosine, sine))
    head, tail = turned

    tails = zero
    for part in range(4):
        end = tail[(part + 2) % 4][:, LANES - 1 : LANES]
        tails = jnp.where(lanes == REACH * part, -end if part < 2 else end, tails)
    tails = jnp.where(last, zero, tails)
    tails_first_ref[...] = jnp.where(first, tails, zero)
    tails_a_ref[...] = jnp.where(jnp.logical_or(first, jnp.logical_not(even)), zero, tails)
    tails_b_ref[...] = jnp.where(even, zero, tails)

    rows = sub_iota()
    packs = []
    for side in range(2):
        blocks = list(turned[side])
        block = jnp.broadcast_to(fields[side][0], (SUBS, LANES))
        for place in range(1, 6):
            block = jnp.where(rows == place, fields[side][place], block)
        blocks.append(block)
        pack = zero
        for part, block in enumerate(blocks):
            shift = REACH * (part + side) % LANES
            moved = pltpu.roll(block, shift, 1) if shift else block
            pack = jnp.where(lanes // REACH == part, moved, pack)
        packs.append(pack)
    pack_a_ref[...] = jnp.where(even, packs[1], packs[0])
    pack_b_ref[...] = jnp.where(even, packs[0], packs[1])

    for copy in moving[7:]:
        copy.wait()


def density_kernel(all_modes, wave_ref, angle_ref, weight_ref, turned_ref, trig_ref, payload_ref):
    tiles = angle_ref.shape[0]
    lanes = lane_iota()
    trig_ref[0] = jnp.cos(angle_ref[...])
    trig_ref[1] = jnp.sin(angle_ref[...])

    weight = weight_ref[...]
    charge_scale = 1.0 / all_modes
    spin_scale = 1.0 / math.sqrt(all_modes)
    nothing = (jnp.zeros((SUBS, LANES), jnp.float32),) * 4

    def rotated(tile):
        if tile == tiles:
            return nothing
        at = slice(tile * LANES, (tile + 1) * LANES)
        cos_row = trig_ref[0, tile : tile + 1, :]
        sin_row = trig_ref[1, tile : tile + 1, :]
        out = rotate_back([wave_ref[part, :, at] for part in range(4)], cos_row, sin_row)
        for part in range(4):
            turned_ref[part, :, at] = out[part]
        return out

    here = rotated(0)
    here_rolled = [shift_from_right(x) for x in here]
    for tile in range(tiles):
        at = slice(tile * LANES, (tile + 1) * LANES)
        after = rotated(tile + 1)
        after_rolled = [shift_from_right(x) for x in after]
        up_real, down_real, up_imag, down_imag = (wave_ref[part, :, at] for part in range(4))
        follow = [jnp.where(lanes == LANES - 1, b, a) for a, b in zip(here_rolled, after_rolled)]
        up_square = up_real * up_real + up_imag * up_imag
        down_square = down_real * down_real + down_imag * down_imag
        current = (
            here[0] * follow[2] + here[1] * follow[3] - here[2] * follow[0] - here[3] * follow[1]
        )
        rows = (
            (up_square + down_square, charge_scale),
            (up_real * down_real + up_imag * down_imag, 2.0 * spin_scale),
            (up_real * down_imag - up_imag * down_real, 2.0 * spin_scale),
            (up_square - down_square, spin_scale),
            (current, 2.0 * spin_scale),
        )
        for place, (value, scale) in enumerate(rows):
            payload_ref[place * tiles + tile : place * tiles + tile + 1, :] = scale * jnp.sum(
                value * weight, axis=0, keepdims=True
            )
        here, here_rolled = after, after_rolled


def region_masks(positions, lead, span, cos_row, sin_row):
    offset = positions - lead
    inside = (offset >= 0.0) & (offset < span)
    zero = jnp.zeros((SUBS, LANES), jnp.float32)
    return jnp.where(inside, cos_row, zero), jnp.where(inside, sin_row, zero)


def setup_kernel(
    scale,
    weight_ref,
    trig_ref,
    potential_ref,
    magnet_ref,
    mask_ref,
    amp_ref,
    group_ref,
    energies_ref,
    lead_ref,
    fields_ref,
    source_ref,
    spin_ref,
    scaled_ref,
):
    tiles = trig_ref.shape[1]
    scaled_ref[...] = scale * weight_ref[...]
    cosine = trig_ref[0]
    sine = trig_ref[1]
    for part in range(3):
        for tile in range(tiles):
            spin_ref[part, tile : tile + 1, :] = magnet_ref[
                part : part + 1, tile * LANES : (tile + 1) * LANES
            ]
    mask = mask_ref[...].astype(jnp.float32)
    strength = exchange_coupling * mask
    field = [strength * spin_ref[part] for part in range(3)]
    for place, value in enumerate(field_rows(potential_ref[...], cosine, sine, field)):
        fields_ref[place] = value
    spin_ref[3] = time_step * mask

    table = (SUBS, energies_ref.shape[1])
    chosen = column(group_ref[...].astype(jnp.float32)) == lax.broadcasted_iota(
        jnp.int32, table, 1
    ).astype(jnp.float32)
    values = jnp.broadcast_to(energies_ref[...], table)
    energy = jnp.sum(jnp.where(chosen, values, jnp.zeros_like(values)), axis=1, keepdims=True)
    energy = jnp.broadcast_to(energy, (SUBS, LANES))
    amps = [
        jnp.broadcast_to(column(amp_ref[part : part + 1, :]), (SUBS, LANES)) for part in range(4)
    ]
    stages = []
    for offset in (0.0, 0.5 * time_step, time_step):
        phase = energy * (start_time + offset)
        cos_phase = jnp.cos(phase)
        sin_phase = jnp.sin(phase)
        stages.append(
            (
                amps[0] * cos_phase + amps[2] * sin_phase,
                amps[1] * cos_phase + amps[3] * sin_phase,
                amps[2] * cos_phase - amps[0] * sin_phase,
                amps[3] * cos_phase - amps[1] * sin_phase,
            )
        )
    first, middle, last = stages
    for part in range(4):
        combined = (
            first[part],
            0.5 * (first[part] + middle[part]),
            (first[part] + 2.0 * middle[part]) * (1.0 / 3.0),
            (first[part] + 4.0 * middle[part] + last[part]) * (1.0 / 6.0),
        )
        for step in range(4):
            source_ref[step * 4 + part] = combined[step]
    source_ref[16] = jnp.broadcast_to(column(lead_ref[...].astype(jnp.float32)), (SUBS, LANES))


def halo_tiles(recv_first_ref, recv_b_ref, recv_a_ref, tiles):
    site_index = lax.axis_index("sites")
    even = lax.rem(site_index, 2) == 0
    inside = {-1: site_index > 0, tiles: site_index < lax.axis_size("sites") - 1}
    halo = {}
    for tile, near_ref, far_ref in ((-1, recv_b_ref, recv_a_ref), (tiles, recv_a_ref, recv_b_ref)):
        pack = jnp.where(even, near_ref[...], far_ref[...])
        pack = jnp.where(site_index == (1 if tile < 0 else 0), recv_first_ref[...], pack)
        pack = jnp.where(inside[tile], pack, jnp.zeros_like(pack))
        start = LANES - REACH if tile < 0 else 0
        blocks = []
        for part in range(5):
            shift = (start - REACH * part) % LANES
            blocks.append(pltpu.roll(pack, shift, 1) if shift else pack)
        halo[tile] = (tuple(blocks[:4]), [blocks[4][place : place + 1, :] for place in range(6)])
    return halo, inside


def one_step(
    step,
    span,
    turned_ref,
    trig_ref,
    fields_ref,
    source_ref,
    halo,
    inside,
    states,
    after_tile=None,
):
    tiles = fields_ref.shape[1]
    lanes = lane_iota()
    first_site = lax.axis_index("sites") * (tiles * LANES)
    lane_position = (lanes + first_site).astype(jnp.float32)
    lead = source_ref[16]
    zero = (jnp.zeros((SUBS, LANES), jnp.float32),) * 4
    (origin_ref, halo_state), target_ref = states
    parts = [source_ref[step * 4 + part] for part in range(4)]
    next_halo = {}

    def load(tile):
        if tile in halo:
            return halo_state[tile]
        if tile > tiles:
            return zero
        return tuple(origin_ref[part, :, tile * LANES : (tile + 1) * LANES] for part in range(4))

    before_up = zero
    here = load(-1)
    here_up = [shift_from_left(x) for x in here]
    here_down = [shift_from_right(x) for x in here]
    for tile in range(-1, tiles + 1):
        after = load(tile + 1)
        after_up = [shift_from_left(x) for x in after]
        after_down = [shift_from_right(x) for x in after]
        if tile not in halo or step < 3:
            if tile in halo:
                base, rows = halo[tile]
            else:
                at = slice(tile * LANES, (tile + 1) * LANES)
                base = tuple(turned_ref[part, :, at] for part in range(4))
                rows = [fields_ref[place, tile : tile + 1, :] for place in range(4)]
                rows += [trig_ref[place, tile : tile + 1, :] for place in range(2)]
            hops = [
                jnp.where(lanes == 0, b, a) + jnp.where(lanes == LANES - 1, d, c)
                for a, b, c, d in zip(here_up, before_up, here_down, after_down)
            ]
            masked = region_masks(lane_position + float(tile * LANES), lead, span, rows[4], rows[5])
            out = horner(base, here, hops, rows[:4], source_terms(parts, *masked), STEP_COEF[step])
            if tile in halo:
                next_halo[tile] = tuple(jnp.where(inside[tile], x, zero[0]) for x in out)
            else:
                if step == 3:
                    out = rotate_fore(out, rows[4], rows[5])
                for part in range(4):
                    target_ref[part, :, at] = out[part]
                if after_tile is not None:
                    after_tile(tile)
        before_up, here, here_up, here_down = here_up, after, after_up, after_down
    return next_halo


def first_steps_kernel(
    span,
    turned_ref,
    trig_ref,
    recv_first_ref,
    recv_b_ref,
    recv_a_ref,
    fields_ref,
    source_ref,
    state_ref,
    halo_ref,
    work_ref,
):
    tiles = fields_ref.shape[1]
    halo, inside = halo_tiles(recv_first_ref, recv_b_ref, recv_a_ref, tiles)
    common = (span, turned_ref, trig_ref, fields_ref, source_ref, halo, inside)
    values = {tile: halo[tile][0] for tile in halo}
    values = one_step(0, *common, ((turned_ref, values), work_ref))
    values = one_step(1, *common, ((work_ref, values), state_ref))
    for side, tile in enumerate((-1, tiles)):
        for part in range(4):
            halo_ref[side, part] = values[tile][part]


def last_steps_kernel(
    span,
    turned_ref,
    trig_ref,
    recv_first_ref,
    recv_b_ref,
    recv_a_ref,
    fields_ref,
    source_ref,
    state_ref,
    halo_ref,
    next_ref,
    work_ref,
    out_ref,
    sems,
):
    tiles = fields_ref.shape[1]
    piece = tiles * LANES // PIECES
    copies = [
        pltpu.make_async_copy(
            out_ref.at[:, :, pl.ds(part * piece, piece)],
            next_ref.at[:, :, pl.ds(part * piece, piece)],
            sems.at[part],
        )
        for part in range(PIECES)
    ]
    halo, inside = halo_tiles(recv_first_ref, recv_b_ref, recv_a_ref, tiles)
    common = (span, turned_ref, trig_ref, fields_ref, source_ref, halo, inside)
    values = {
        tile: tuple(halo_ref[side, part] for part in range(4))
        for side, tile in enumerate((-1, tiles))
    }
    values = one_step(2, *common, ((state_ref, values), work_ref))

    def after_tile(tile):
        if (tile + 1) * LANES % piece == 0:
            copies[tile * LANES // piece].start()

    one_step(3, *common, ((work_ref, values), out_ref), after_tile)
    for copy in copies:
        copy.wait()


def finish_kernel(
    own_ref,
    other_ref,
    corner_ref,
    corner_other_ref,
    spin_ref,
    densities_ref,
    magnet_next_ref,
    densities_out,
    magnet_out,
    sems,
):
    tiles = spin_ref.shape[1]
    copies = [
        pltpu.make_async_copy(densities_out, densities_ref, sems.at[0]),
        pltpu.make_async_copy(magnet_out, magnet_next_ref, sems.at[1]),
    ]
    totals = []
    for place in range(5):
        rows = slice(place * tiles, (place + 1) * tiles)
        totals.append(own_ref[rows, :] + other_ref[rows, :])
    products = corner_ref[...] + corner_other_ref[...]
    corner = jnp.sum(jnp.sum(products, axis=1, keepdims=True), axis=0, keepdims=True)
    row_at = lax.broadcasted_iota(jnp.int32, (tiles, LANES), 0)
    lane_at = lax.broadcasted_iota(jnp.int32, (tiles, LANES), 1)
    totals[4] = jnp.where((row_at == tiles - 1) & (lane_at == LANES - 1), corner, totals[4])
    for place in range(5):
        for tile in range(tiles):
            densities_out[place : place + 1, tile * LANES : (tile + 1) * LANES] = totals[place][
                tile : tile + 1, :
            ]
    copies[0].start()
    field_x, field_y, field_z = (exchange_coupling * totals[1 + part] for part in range(3))
    magnet_x, magnet_y, magnet_z = (spin_ref[part] for part in range(3))
    torque = (
        magnet_y * field_z - magnet_z * field_y,
        magnet_z * field_x - magnet_x * field_z,
        magnet_x * field_y - magnet_y * field_x,
    )
    for part, magnet in enumerate((magnet_x, magnet_y, magnet_z)):
        advanced = magnet - spin_ref[3] * torque[part]
        for tile in range(tiles):
            magnet_out[part : part + 1, tile * LANES : (tile + 1) * LANES] = advanced[
                tile : tile + 1, :
            ]
    copies[1].start()
    for copy in copies:
        copy.wait()


def local(
    wave_state,
    potential,
    spin_angle,
    magnet,
    magnetic_mask,
    mode_weight,
    source_amp,
    mode_group,
    energies,
    lead_site,
):
    local_modes, local_sites = wave_state.shape[1:]
    site_count = lax.axis_size("sites")
    mode_count = lax.axis_size("modes")
    assert local_modes == SUBS and local_sites % (LANES * PIECES) == 0
    tiles = local_sites // LANES
    span = float(local_sites * site_count // 8)
    f32 = jnp.float32
    vmem = pl.BlockSpec(memory_space=pltpu.VMEM)
    anywhere = pl.BlockSpec(memory_space=pl.ANY)
    dense = (tiles, LANES)
    kept = lambda array: pltpu.with_memory_space_constraint(array, pltpu.VMEM)

    potential = potential.reshape(dense)
    spin_angle = spin_angle.reshape(dense)
    magnetic_mask = magnetic_mask.reshape(dense)

    row = lambda array: array.reshape(1, -1)
    small = (row(mode_weight), source_amp, row(mode_group), row(energies), row(lead_site))
    site_arrays = (potential, magnet, magnetic_mask)
    (pack_a, pack_b, tails_first, tails_a, tails_b, weight, *staged, angle_staged) = pl.pallas_call(
        edge_kernel,
        out_shape=(
            *(pltpu.VMEM((SUBS, LANES), f32) for _ in range(6)),
            *(pltpu.VMEM(array.shape, array.dtype) for array in site_arrays + small[1:]),
            pltpu.VMEM(dense, f32),
        ),
        in_specs=[anywhere] * 10,
        out_specs=[vmem] * 14,
        scratch_shapes=[
            pltpu.VMEM((2, 4, SUBS, LANES), f32),
            pltpu.VMEM(small[0].shape, f32),
            pltpu.SemaphoreType.DMA((11,)),
        ],
        name="edges",
        cost_estimate=pl.CostEstimate(flops=100_000, bytes_accessed=200_000, transcendentals=0),
    )(wave_state, potential, spin_angle, magnet, magnetic_mask, *small)

    wave_late, pack_b = lax.optimization_barrier((wave_state, pack_b))
    turned, trig, payload = pl.pallas_call(
        functools.partial(density_kernel, local_modes * mode_count),
        out_shape=(
            pltpu.VMEM(wave_state.shape, f32),
            pltpu.VMEM((2,) + dense, f32),
            pltpu.VMEM((5 * tiles, LANES), f32),
        ),
        in_specs=[vmem] * 3,
        out_specs=[vmem] * 3,
        name="densities",
        cost_estimate=pl.CostEstimate(flops=10_000_000, bytes_accessed=1_500_000, transcendentals=0),
    )(kept(wave_late), kept(angle_staged), kept(weight))

    def swap_sites(pack, pairs):
        partner = {i: j for pair in pairs for i, j in (pair, pair[::-1])}
        whole = [
            (
                m * site_count + s,
                m * site_count + partner[s] if s in partner else (m ^ 1) * site_count + s,
            )
            for m in range(mode_count)
            for s in range(site_count)
        ]
        return lax.ppermute(pack, ("modes", "sites"), whole)

    def swap_modes(array, distance):
        return lax.ppermute(array, "modes", [(i, i ^ distance) for i in range(mode_count)])

    recv_b = swap_sites(pack_b, [(i, i + 1) for i in range(1, site_count - 1, 2)])
    recv_a = swap_sites(pack_a, [(i, i + 1) for i in range(2, site_count - 1, 2)])
    recv_first = swap_sites(pack_a, [(0, 1)])
    distance = 1
    while 2 * distance < mode_count:
        payload = payload + swap_modes(payload, distance)
        distance *= 2
    last_distance = distance + 1 if distance > 1 else distance
    payload, weight = lax.optimization_barrier((payload, weight))
    payload_other = swap_modes(payload, last_distance)

    fields, source, spin, scaled = pl.pallas_call(
        functools.partial(setup_kernel, 2.0 / math.sqrt(local_modes * mode_count)),
        out_shape=(
            pltpu.VMEM((4,) + dense, f32),
            pltpu.VMEM((17, SUBS, LANES), f32),
            pltpu.VMEM((4,) + dense, f32),
            pltpu.VMEM((SUBS, LANES), f32),
        ),
        in_specs=[vmem] * 9,
        out_specs=[vmem] * 4,
        name="setup",
        cost_estimate=pl.CostEstimate(flops=1_000_000, bytes_accessed=200_000, transcendentals=0),
    )(kept(weight), kept(trig), *(kept(array) for array in staged))

    product = scaled * (tails_first * recv_first + tails_b * recv_b + tails_a * recv_a)
    distance = 1
    while 2 * distance < mode_count:
        product = product + swap_modes(product, distance)
        distance *= 2
    common = (turned, trig, recv_first, recv_b, recv_a, fields, source)
    state, halo_state = pl.pallas_call(
        functools.partial(first_steps_kernel, span),
        out_shape=(
            pltpu.VMEM(wave_state.shape, f32),
            pltpu.VMEM((2, 4, SUBS, LANES), f32),
        ),
        in_specs=[vmem] * 7,
        out_specs=[vmem] * 2,
        scratch_shapes=[pltpu.VMEM(wave_state.shape, f32)],
        name="first_steps",
        cost_estimate=pl.CostEstimate(flops=10_000_000, bytes_accessed=700_000, transcendentals=0),
    )(*(kept(array) for array in common))
    product, halo_state = lax.optimization_barrier((product, halo_state))
    product_other = swap_modes(product, last_distance)


    next_state = pl.pallas_call(
        functools.partial(last_steps_kernel, span),
        out_shape=jax.ShapeDtypeStruct(wave_state.shape, f32),
        in_specs=[vmem] * (len(common) + 2),
        out_specs=anywhere,
        scratch_shapes=[
            pltpu.VMEM(wave_state.shape, f32),
            pltpu.VMEM(wave_state.shape, f32),
            pltpu.SemaphoreType.DMA((PIECES,)),
        ],
        name="last_steps",
        cost_estimate=pl.CostEstimate(flops=10_000_000, bytes_accessed=700_000, transcendentals=0),
    )(*(kept(array) for array in common + (state, halo_state)))

    densities, magnet_next = pl.pallas_call(
        finish_kernel,
        out_shape=(
            jax.ShapeDtypeStruct((5, local_sites), f32),
            jax.ShapeDtypeStruct((3, local_sites), f32),
        ),
        in_specs=[vmem] * 5,
        out_specs=[anywhere] * 2,
        scratch_shapes=[
            pltpu.VMEM((5, local_sites), f32),
            pltpu.VMEM((3, local_sites), f32),
            pltpu.SemaphoreType.DMA((2,)),
        ],
        name="finish",
        cost_estimate=pl.CostEstimate(flops=1_000_000, bytes_accessed=400_000, transcendentals=0),
    )(kept(payload), kept(payload_other), kept(product), kept(product_other), kept(spin))
    return (next_state, densities, magnet_next)


def solution(mesh):
    return jax.shard_map(
        local,
        mesh=mesh,
        in_specs=(
            P(None, "modes", "sites"),
            P("sites"),
            P("sites"),
            P(None, "sites"),
            P("sites"),
            P("modes"),
            P(None, "modes"),
            P("modes"),
            P(),
            P("modes"),
        ),
        out_specs=(P(None, "modes", "sites"), P(None, "sites"), P(None, "sites")),
        check_vma=False,
    )
```
